32 devices in a mesh: row: 4 (over x, core), col: 8 (over z, y).
Axes of the slice: x: 2, y: 2, z: 4, core: 2. Of those that a mesh axis runs over, the one named last changes fastest.
Arguments:
- dinv_root: bfloat16 [16384, 16384], P('row', 'col'), may hold values from -0.03125 to 0.03125
- rhs_root: bfloat16 [16384, 384], P('col'), may hold values from -6 to 6
- dinv_mid: bfloat16 [16384, 8192], P('row', 'col'), may hold values from -0.046875 to 0.046875
- coup_mid: bfloat16 [16384, 8192], P('row', 'col'), may hold values from -0.0625 to 0.0625
- rhs_mid: bfloat16 [2, 8192, 384], P(None, 'col'), may hold values from -6 to 6
- dinv_leaf: bfloat16 [8, 4096, 4096], P('col', None, 'row'), may hold values from -0.0625 to 0.0625
- coup_leaf: bfloat16 [8, 6144, 4096], P('col', 'row'), may hold values from -0.109375 to 0.109375
- rhs_leaf: bfloat16 [8, 4096, 384], P('col', 'row'), may hold values from -6 to 6
- bounds_mid: int32 [2, 64], replicated, may hold values from 0 to 127, as said below
- bounds_leaf: int32 [8, 48], replicated, may hold values from 0 to 191, as said below
- parents: int32 [8], replicated, may hold values from 0 to 1, as said below
Outputs:
- root_values: bfloat16 [16384, 384], P(('row', 'col'))
- mid_values: bfloat16 [16384, 384], P(('row', 'col'))
- leaf_values: bfloat16 [8, 4096, 384], P('col', 'row')
The draws below stay inside these ranges and needn't reach their ends.
Inputs may be any that keep to these rules, and one draw needn't show every extreme that they name: `bounds_mid`: each row holds 64 distinct root block numbers; every root block appears in some row. `parents`: each mid front is the parent of exactly 4 leaf fronts. `bounds_leaf`: each row holds 48 distinct values. Every row names the same number of root blocks; the leaf fronts of one parent together name each block of that parent's separator exactly once, each naming 8192 / 128 / 4 of them.
All inputs are finite; a program needn't handle non-finite values.
Results may differ from the reference program's by a relative error of at most 0.0065.
Values may be sent and summed in bfloat16 or wider, within the bound.
No kernel may reach another device: no remote copies, remote signals or barrier semaphores. Data moves between devices by JAX's collectives and lax.ppermute only.
A program may use at most 128 MiB of HBM per device.

```python
import jax
import jax.numpy as jnp
from jax import lax

N0 = 16384
N1 = 8192
N2 = 4096
B1 = 8192
B2 = 6144
BLOCK = 128
RHS = 384
F1 = 2
F2 = 8


def draw_bounds_mid(key, part):
    root_total = N0 // BLOCK
    list_len = B1 // BLOCK
    root_order = jax.random.permutation(jax.random.fold_in(key, 3), root_total).astype(jnp.int32)
    stride = root_total // F1

    def front_list(front_id):
        positions = (front_id * stride + jnp.arange(list_len, dtype=jnp.int32)) % root_total
        shuffle = jax.random.permutation(jax.random.fold_in(key, 200 + front_id), list_len)
        return root_order[positions][shuffle]
    return jax.vmap(front_list)(jnp.arange(F1, dtype=jnp.int32)).astype(jnp.int32)


def leaf_tables(key):
    base_key = jax.random.fold_in(key, 11)
    slot_order = jax.random.permutation(jax.random.fold_in(base_key, 1), F2).astype(jnp.int32)
    fan_out = F2 // F1
    parent_ids = slot_order // fan_out
    ordinal = slot_order % fan_out
    parent_total = N1 // BLOCK
    per_child = parent_total // fan_out
    root_total = N0 // BLOCK
    root_take = B2 // BLOCK - per_child
    root_order = jax.random.permutation(jax.random.fold_in(base_key, 2), root_total).astype(jnp.int32)
    stride = root_total // F2

    def parent_deal(parent_id):
        return jax.random.permutation(jax.random.fold_in(base_key, 300 + parent_id), parent_total).astype(jnp.int32)
    parent_orders = jax.vmap(parent_deal)(jnp.arange(F1, dtype=jnp.int32))

    def child_list(slot_id):
        positions = (slot_id * stride + jnp.arange(root_take, dtype=jnp.int32)) % root_total
        root_pick = root_order[positions]
        dealt = parent_orders[parent_ids[slot_id]]
        own_part = root_total + dealt[ordinal[slot_id] * per_child + jnp.arange(per_child, dtype=jnp.int32)]
        entries = jnp.concatenate([root_pick, own_part])
        shuffle = jax.random.permutation(jax.random.fold_in(base_key, 100 + slot_id), B2 // BLOCK)
        return entries[shuffle]
    all_lists = jax.vmap(child_list)(jnp.arange(F2, dtype=jnp.int32))
    return (parent_ids.astype(jnp.int32), all_lists.astype(jnp.int32))


def draw_bounds_leaf(key, part):
    return leaf_tables(key)[1]


def draw_parents(key, part):
    return leaf_tables(key)[0]


def strengthened(drawn, stream_key, source, target, shards_of, factor):
    def block_of(position):
        return (jnp.arange(drawn.shape[position]) // (drawn.shape[position] // shards_of)).reshape((-1,) + (1,) * (drawn.ndim - 1 - position))

    one_side = jax.random.permutation(stream_key, shards_of)[block_of(target)]
    second = (block_of(target) + shards_of // 2) % shards_of
    return jnp.where((block_of(source) == one_side) | (block_of(source) == second), factor * drawn, drawn)


def levels(own_key, dims, shards, low, high):
    factor_of = 1.0
    for position, shards_of in shards:
        heights = jax.random.uniform(jax.random.fold_in(jax.random.fold_in(own_key, 6), position), (shards_of,), jnp.float32, low / len(shards), high / len(shards))
        factor_of = factor_of * jnp.repeat(jnp.exp(heights), dims[position] // shards_of).reshape((-1,) + (1,) * (len(dims) - 1 - position))
    return factor_of


def scatter_about(key, extent, deviation, reach, shards=(), kind=jnp.bfloat16):
    values = jax.random.normal(key, extent, jnp.float32) * deviation
    if len(shards) > 0:
        values = levels(key, extent, shards, -0.22, 0.18) * values
    return jnp.clip(values, min=-reach, max=reach).astype(kind)


def bell_draw_with(key, shape, width, reach, cuts, heavy, kind=jnp.bfloat16):
    drawn = width * jax.random.normal(key, shape, jnp.float32)
    if cuts:
        drawn = drawn * levels(key, shape, cuts, -0.22, 0.18)
    return jnp.clip(strengthened(drawn, jax.random.fold_in(key, 3), *heavy), -reach, reach).astype(kind)


def setup_inputs(seed: int = 0) -> dict:
    keys = jax.random.split(jax.random.key(seed), 12)
    return {
        "dinv_root": bell_draw_with(keys[0], (N0, N0), (4 * N0) ** -0.5, 0.03125, ((0, 4), (1, 8)), (1, 0, 8, 2.0)),
        "rhs_root": scatter_about(keys[1], (N0, RHS), 1.0, 6.0, ((0, 8),)),
        "dinv_mid": bell_draw_with(keys[2], (F1 * N1, N1), (4 * N1) ** -0.5, 0.046875, ((0, 4), (1, 8)), (1, 0, 8, 2.0)),
        "coup_mid": scatter_about(keys[3], (F1 * B1, N1), B1 ** -0.5, 0.0625, ((0, 4), (1, 8))),
        "rhs_mid": scatter_about(keys[4], (F1, N1, RHS), 1.0, 6.0, ((1, 8),)),
        "dinv_leaf": bell_draw_with(keys[5], (F2, N2, N2), (4 * N2) ** -0.5, 0.0625, ((0, 8), (2, 4)), (2, 1, 4, 2.0)),
        "coup_leaf": bell_draw_with(keys[6], (F2, B2, N2), B2 ** -0.5, 0.109375, ((0, 8), (1, 4)), (1, 2, 4, 2.0)),
        "rhs_leaf": scatter_about(keys[7], (F2, N2, RHS), 1.0, 6.0, ((0, 8), (1, 4))),
        "bounds_mid": draw_bounds_mid(jax.random.fold_in(keys[11], 71), 0),
        "bounds_leaf": draw_bounds_leaf(jax.random.fold_in(keys[11], 71), 0),
        "parents": draw_parents(jax.random.fold_in(keys[11], 71), 0),
    }


def reference(dinv_root, rhs_root, dinv_mid, coup_mid, rhs_mid, dinv_leaf, coup_leaf, rhs_leaf, bounds_mid, bounds_leaf, parents):
    rhs_width = rhs_root.shape[1]
    root_values = jnp.dot(dinv_root, rhs_root, preferred_element_type=jnp.float32).astype(jnp.bfloat16)
    root_blocks = root_values.reshape(N0 // BLOCK, BLOCK, rhs_width)

    def mid_front(front_id):
        boundary = root_blocks[bounds_mid[front_id]].reshape(B1, rhs_width)
        coupling = lax.dynamic_slice_in_dim(coup_mid, front_id * B1, B1, 0)
        terms = jnp.dot(coupling.T, boundary, preferred_element_type=jnp.float32)
        shifted = (rhs_mid[front_id].astype(jnp.float32) - terms).astype(jnp.bfloat16)
        inverse = lax.dynamic_slice_in_dim(dinv_mid, front_id * N1, N1, 0)
        return jnp.dot(inverse, shifted, preferred_element_type=jnp.float32).astype(jnp.bfloat16)

    mid_stack = lax.map(mid_front, jnp.arange(F1, dtype=jnp.int32))
    mid_values = mid_stack.reshape(F1 * N1, rhs_width)

    def leaf_front(slot_id):
        parent_blocks = mid_stack[parents[slot_id]].reshape(N1 // BLOCK, BLOCK, rhs_width)
        sources = jnp.concatenate([root_blocks, parent_blocks], axis=0)
        boundary = sources[bounds_leaf[slot_id]].reshape(B2, rhs_width)
        terms = jnp.dot(coup_leaf[slot_id].T, boundary, preferred_element_type=jnp.float32)
        shifted = (rhs_leaf[slot_id].astype(jnp.float32) - terms).astype(jnp.bfloat16)
        return jnp.dot(dinv_leaf[slot_id], shifted, preferred_element_type=jnp.float32).astype(jnp.bfloat16)

    leaf_values = lax.map(leaf_front, jnp.arange(F2, dtype=jnp.int32))
    return root_values, mid_values, leaf_values
```

```python
import functools

import jax
import jax.numpy as jnp
from jax import lax
from jax.experimental import pallas as pl
from jax.experimental.pallas import tpu as pltpu
from jax.sharding import PartitionSpec as P

BLOCK = 128
CHUNKS = 3
F32 = jnp.float32
BF16 = jnp.bfloat16
NT = (((1,), (1,)), ((), ()))
NN = (((1,), (0,)), ((), ()))


def partner(value, axis, distance):
    mask = 2**distance
    pairs = [(source, source ^ mask) for source in range(lax.axis_size(axis))]
    return lax.ppermute(value, axis, pairs)


def pick_blocks(shard_rows, wanted):
    block_count = shard_rows.shape[0] // BLOCK
    flat_blocks = shard_rows.reshape(block_count, BLOCK * shard_rows.shape[1])
    present = jnp.arange(block_count, dtype=jnp.int32)
    select = (wanted[:, None] == present[None, :]).astype(shard_rows.dtype)
    return jnp.dot(select, flat_blocks, preferred_element_type=F32)


def transposed_product(coupling, boundary):
    return lax.dot_general(coupling, boundary, (((0,), (0,)), ((), ())), preferred_element_type=F32)


def general_shards(
    dinv_root,
    rhs_root,
    dinv_mid,
    coup_mid,
    rhs_mid,
    dinv_leaf,
    coup_leaf,
    rhs_leaf,
    bounds_mid,
    bounds_leaf,
    parents,
):
    row_total = lax.axis_size("row")
    row_id = lax.axis_index("row")
    col_id = lax.axis_index("col")
    rhs_width = rhs_root.shape[1]
    root_total = dinv_root.shape[0] * row_total // BLOCK
    front_mid = row_id // 2
    half_index = row_id % 2
    half_blocks = bounds_mid.shape[1] // 2
    mid_all = lax.dynamic_slice_in_dim(bounds_mid, front_mid, 1, 0)[0]
    mid_list = lax.dynamic_slice_in_dim(mid_all, half_index * half_blocks, half_blocks, 0)
    leaf_all = lax.dynamic_slice_in_dim(bounds_leaf, col_id, 1, 0)[0]
    leaf_slots = leaf_all.shape[0] // row_total
    leaf_list = lax.dynamic_slice_in_dim(leaf_all, row_id * leaf_slots, leaf_slots, 0)
    wanted = jnp.concatenate([mid_list, leaf_list])
    root_values = lax.psum_scatter(
        jnp.dot(dinv_root, rhs_root, preferred_element_type=F32),
        "col",
        scatter_dimension=0,
        tiled=True,
    ).astype(BF16)
    picked = pick_blocks(lax.all_gather(root_values, ("row", "col"), axis=0, tiled=True), wanted)
    bound_mid = picked[:half_blocks].reshape(half_blocks * BLOCK, rhs_width).astype(BF16)
    root_side = picked[half_blocks:]
    mid_part = transposed_product(coup_mid, bound_mid)
    mid_terms = mid_part + partner(mid_part, "row", 0)
    rhs_here = lax.dynamic_slice_in_dim(rhs_mid, front_mid, 1, 0)[0]
    shift_mid = (rhs_here - mid_terms).astype(BF16)
    mid_values = lax.psum_scatter(
        jnp.dot(dinv_mid, shift_mid, preferred_element_type=F32),
        "col",
        scatter_dimension=0,
        tiled=True,
    ).astype(BF16)
    half_rows = lax.all_gather(mid_values, "col", axis=0, tiled=True)
    half_count = half_rows.shape[0] // BLOCK
    half_flat = half_rows.reshape(half_count, BLOCK * rhs_width)
    local_ids = leaf_all - root_total - half_index * half_count
    owns_parent = lax.dynamic_slice_in_dim(parents, col_id, 1, 0)[0] == front_mid
    choose = (
        (local_ids[:, None] == jnp.arange(half_count, dtype=jnp.int32)[None, :]) & owns_parent
    ).astype(BF16)
    from_parent = lax.psum_scatter(
        jnp.dot(choose, half_flat, preferred_element_type=F32).astype(BF16),
        "row",
        scatter_dimension=0,
        tiled=True,
    ).astype(F32)
    bound_leaf = (root_side + from_parent).reshape(leaf_slots * BLOCK, rhs_width).astype(BF16)
    leaf_sum = lax.psum_scatter(
        transposed_product(coup_leaf[0], bound_leaf), "row", scatter_dimension=0, tiled=True
    )
    shift_leaf = (rhs_leaf[0] - leaf_sum).astype(BF16)
    leaf_values = lax.psum_scatter(
        jnp.dot(dinv_leaf[0], shift_leaf, preferred_element_type=F32),
        "row",
        scatter_dimension=0,
        tiled=True,
    ).astype(BF16)
    return (root_values, mid_values, leaf_values[None])


SMEM = pl.BlockSpec(memory_space=pltpu.SMEM)
VMEM = pl.BlockSpec(memory_space=pltpu.VMEM)
LIMIT = 48 * 1024 * 1024


def params():
    return pltpu.CompilerParams(vmem_limit_bytes=LIMIT)


def loop(count, body):
    def step(i, carry):
        body(i)
        return carry

    lax.fori_loop(0, count, step, 0)


def mark_fronts(bounds_ref, front):
    def body(j):
        front[bounds_ref[0, j]] = 0
        front[bounds_ref[1, j]] = 1

    loop(bounds_ref.shape[1], body)


def order_kernel(local, slot, place_ref, bounds_ref, out_ref, front):
    x, h, z, y = (place_ref[i] for i in range(4))
    first = (2 * x + h) * local
    mark_fronts(bounds_ref, front)
    before = lax.fori_loop(0, first, lambda v, s: s + 1 - front[v], jnp.int32(0))
    zeros = lax.fori_loop(0, local, lambda i, s: s + 1 - front[first + i], jnp.int32(0))

    def body(i, carry):
        low, high = carry
        kind = front[first + i]
        rank = jnp.where(kind == 0, low, zeros + high)
        chip = (before + rank) & 7
        near = ((chip & 1) ^ y) * (local // 2) + ((chip >> 1) ^ z) * slot
        out_ref[near + (rank >> 3)] = i
        return low + 1 - kind, high + kind

    lax.fori_loop(0, local, body, (jnp.int32(0), jnp.int32(0)))


def plan_kernel(local, slot, leaf_slots, place_ref, bounds_ref, leaf_ref, parents_ref, out_ref, front, ident, where):
    x, h, z, y = (place_ref[i] for i in range(4))
    col = 2 * z + y
    total = 4 * local
    mark_fronts(bounds_ref, front)

    def per_row(r, before):
        zeros = lax.fori_loop(0, local, lambda i, s: s + 1 - front[r * local + i], jnp.int32(0))

        def body(i, carry):
            low, high = carry
            kind = front[r * local + i]
            rank = jnp.where(kind == 0, low, zeros + high)
            chip = (before + rank) & 7
            ident[r * local + chip * slot + (rank >> 3)] = r * local + i
            return low + 1 - kind, high + kind

        lax.fori_loop(0, local, body, (jnp.int32(0), jnp.int32(0)))
        return before + zeros

    lax.fori_loop(0, 4, per_row, jnp.int32(0))

    def clear(v):
        where[v] = 0

    loop(total, clear)

    def per_chip(chip, _):
        here = chip == col
        near = ((chip & 1) ^ y) * (local // 2) + ((chip >> 1) ^ z) * slot

        def put(core, count, block, code):
            where[block] = (core ^ h) * local + near + count

            @pl.when(here & (core == h))
            def _():
                out_ref[count] = code

        def from_far(step, carry):
            count0, count1 = carry
            core, k = step // slot, step % slot
            block = ident[(2 * (1 - x) + core) * local + chip * slot + k]
            taken = front[block] == x
            count = jnp.where(core == 0, count0, count1)

            @pl.when(taken)
            def _():
                put(core, count, block, 2 * slot + k)

            add = taken.astype(jnp.int32)
            return count0 + jnp.where(core == 0, add, 0), count1 + jnp.where(core == 0, 0, add)

        counts = lax.fori_loop(0, 2 * slot, from_far, (jnp.int32(0), jnp.int32(0)))

        def from_near(step, carry):
            count0, count1 = carry
            owner, k = step // slot, step % slot
            block = ident[(2 * x + owner) * local + chip * slot + k]
            taken = front[block] == x
            core = (count0 >= slot).astype(jnp.int32)
            count = jnp.where(core == 0, count0, count1)

            @pl.when(taken)
            def _():
                put(core, count, block, (owner ^ core) * slot + k)

            add = taken.astype(jnp.int32)
            return count0 + jnp.where(core == 0, add, 0), count1 + jnp.where(core == 0, 0, add)

        lax.fori_loop(0, 2 * slot, from_near, counts)
        return 0

    lax.fori_loop(0, 8, per_chip, 0)

    at = plan_layout(local, slot, leaf_slots)

    def mid_place(block):
        inner = block % local
        chip = inner // slot
        near = ((chip & 1) ^ y) * (local // 2) + ((chip >> 1) ^ z) * slot
        return ((block // local) ^ h) * local + near + inner % slot

    def mid_list(j):
        out_ref[at["mid"] + j] = where[bounds_ref[x, h * local + j]]

    loop(local, mid_list)
    far = 2 * (1 - x) + h
    mine = 2 * x + h
    owner = parents_ref[col] == x

    def lists(j):
        asked = leaf_ref[col, far * leaf_slots + j]
        out_ref[at["send_root"] + j] = where[jnp.minimum(asked, total - 1)]
        out_ref[at["send_mid"] + j] = mid_place(jnp.maximum(asked - total, 0))
        held = leaf_ref[col, mine * leaf_slots + j]
        low = jnp.minimum(held, total - 1)
        from_root = jnp.where(front[low] == x, where[low], 2 * local + j)
        from_mid = jnp.where(owner, mid_place(jnp.maximum(held - total, 0)), 2 * local + j) + at["mid_base"]
        out_ref[at["leaf"] + j] = jnp.where(held < total, from_root, from_mid)

    loop(leaf_slots, lists)

    def outs(j):
        asked = far * local + col * slot + j
        out_ref[at["send_root"] + leaf_slots + j] = where[asked]
        held = mine * local + col * slot + j
        out_ref[at["out"] + j] = jnp.where(front[held] == x, where[held], 2 * local + leaf_slots + j)

    loop(slot, outs)


def plan_layout(local, slot, leaf_slots):
    at = {}
    size = 0
    for name, count in (
        ("select", slot),
        ("mid", local),
        ("send_root", leaf_slots + slot),
        ("leaf", leaf_slots),
        ("out", slot),
        ("send_mid", leaf_slots),
    ):
        at[name] = size
        size += count
    at["size"] = size
    at["mid_base"] = 2 * local + leaf_slots + slot
    return at


def fetch(sources, code, target, index):
    base = 0
    for source in sources:
        count = source.shape[0]

        @pl.when((code >= base) & (code < base + count))
        def _(source=source, base=base):
            target[index] = source[code - base]

        base += count


def gather_kernel(start, count, table_ref, *refs):
    *sources, out_ref = refs
    for i in range(count):
        fetch(sources, table_ref[start + i], out_ref, i)


def gather(table, start, count, *sources):
    shape = sources[0].shape
    return pl.pallas_call(
        functools.partial(gather_kernel, start, count),
        out_shape=jax.ShapeDtypeStruct((count,) + shape[1:], BF16),
        in_specs=[SMEM] + [VMEM] * len(sources),
        out_specs=VMEM,
        compiler_params=params(),
    )(table, *sources)


def row_product_kernel(parts, order_ref, value_ref, *refs):
    *blocks, out_ref = refs
    matrix = jnp.concatenate([b[...] for b in blocks], axis=0)
    result = lax.dot_general(value_ref[...], matrix, NT, preferred_element_type=F32).astype(BF16)
    for i in range(parts):
        out_ref[i] = result[:, i * BLOCK : (i + 1) * BLOCK]


def row_product(order, start, count, value, matrix, parts=4):
    width, depth = value.shape

    def spec(i):
        return pl.BlockSpec((BLOCK, depth), lambda s, order: (order[start + parts * s + i], 0))

    return pl.pallas_call(
        functools.partial(row_product_kernel, parts),
        grid_spec=pltpu.PrefetchScalarGridSpec(
            num_scalar_prefetch=1,
            grid=(count // parts,),
            in_specs=[pl.BlockSpec((width, depth), lambda s, order: (0, 0))] + [spec(i) for i in range(parts)],
            out_specs=pl.BlockSpec((parts, width, BLOCK), lambda s, order: (s, 0, 0)),
        ),
        out_shape=jax.ShapeDtypeStruct((count, width, BLOCK), BF16),
        compiler_params=params(),
        cost_estimate=pl.CostEstimate(
            flops=2 * count * BLOCK * depth * width, bytes_accessed=2 * count * BLOCK * depth, transcendentals=0
        ),
    )(order, value, *([matrix] * parts))


def mid_coupling_kernel(start, parts, table_ref, own_ref, sib_ref, coup_ref, out_ref, bound):
    step = pl.program_id(0)
    for i in range(parts):
        fetch([own_ref, sib_ref], table_ref[start + parts * step + i], bound, i)
    value = jnp.concatenate([bound[i] for i in range(parts)], axis=1)
    product = lax.dot_general(value, coup_ref[...], NN, preferred_element_type=F32)

    @pl.when(step == 0)
    def _():
        out_ref[...] = product

    @pl.when(step > 0)
    def _():
        out_ref[...] += product


def mid_coupling(table, start, own, sib, coup, parts=4):
    local, width, _ = own.shape
    rows, cols = coup.shape
    whole = pl.BlockSpec((local, width, BLOCK), lambda s, table: (0, 0, 0))
    return pl.pallas_call(
        functools.partial(mid_coupling_kernel, start, parts),
        grid_spec=pltpu.PrefetchScalarGridSpec(
            num_scalar_prefetch=1,
            grid=(local // parts,),
            in_specs=[whole, whole, pl.BlockSpec((parts * BLOCK, cols), lambda s, table: (s, 0))],
            out_specs=pl.BlockSpec((width, cols), lambda s, table: (0, 0)),
            scratch_shapes=[pltpu.VMEM((parts, width, BLOCK), BF16)],
        ),
        out_shape=jax.ShapeDtypeStruct((width, cols), F32),
        compiler_params=params(),
        cost_estimate=pl.CostEstimate(
            flops=2 * rows * cols * width, bytes_accessed=2 * rows * cols, transcendentals=0
        ),
    )(table, own, sib, coup)


def leaf_coupling_kernel(order_ref, bound_ref, coup_ref, out_ref):
    out_ref[0] = lax.dot_general(bound_ref[...], coup_ref[...], NN, preferred_element_type=F32).astype(BF16)


def leaf_coupling(order, start, count, bound, coup, cols):
    width, depth = bound.shape
    return pl.pallas_call(
        leaf_coupling_kernel,
        grid_spec=pltpu.PrefetchScalarGridSpec(
            num_scalar_prefetch=1,
            grid=(count,),
            in_specs=[
                pl.BlockSpec((width, depth), lambda s, order: (0, 0)),
                pl.BlockSpec((depth, cols), lambda s, order: (0, order[start + s])),
            ],
            out_specs=pl.BlockSpec((1, width, cols), lambda s, order: (s, 0, 0)),
        ),
        out_shape=jax.ShapeDtypeStruct((count, width, cols), BF16),
        compiler_params=params(),
        cost_estimate=pl.CostEstimate(
            flops=2 * count * depth * cols * width, bytes_accessed=2 * count * depth * cols, transcendentals=0
        ),
    )(order, bound, coup)


def leaf_inverse_kernel(order_ref, value_ref, matrix_ref, out_ref):
    out_ref[0] = lax.dot_general(value_ref[...], matrix_ref[...], NT, preferred_element_type=F32).astype(BF16)


def leaf_inverse(order, start, count, value, matrix):
    width, depth = value.shape
    rows = depth
    return pl.pallas_call(
        leaf_inverse_kernel,
        grid_spec=pltpu.PrefetchScalarGridSpec(
            num_scalar_prefetch=1,
            grid=(count,),
            in_specs=[
                pl.BlockSpec((width, depth), lambda s, order: (0, 0)),
                pl.BlockSpec((rows, depth), lambda s, order: (order[start + s], 0)),
            ],
            out_specs=pl.BlockSpec((1, width, rows), lambda s, order: (s, 0, 0)),
        ),
        out_shape=jax.ShapeDtypeStruct((count, width, rows), BF16),
        compiler_params=params(),
        cost_estimate=pl.CostEstimate(
            flops=2 * count * rows * depth * width, bytes_accessed=2 * count * rows * depth, transcendentals=0
        ),
    )(order, value, matrix)


def swap(value, axis, mask):
    return lax.ppermute(value, axis, [(i, i ^ mask) for i in range(lax.axis_size(axis))])


def add(*terms):
    return functools.reduce(jnp.add, [t.astype(F32) for t in terms])


def reduce_columns(send, keep, slot):
    got = swap(send, "col", 1)
    part = [add(keep[m * slot : (m + 1) * slot], got[m * slot : (m + 1) * slot]) for m in range(4)]
    far = [swap(part[m].astype(BF16), "col", 2 * m) for m in (1, 2, 3)]
    return add(part[0], *far).astype(BF16)


def gather_columns(value):
    far = [swap(value, "col", 2 * m) for m in (1, 2, 3)]
    near = swap(value, "col", 1)
    rest = jnp.concatenate(far, axis=0)
    return jnp.concatenate([value, rest, near, swap(rest, "col", 1)], axis=0)


def natural(blocks):
    return jnp.swapaxes(blocks, 1, 2).reshape(-1, blocks.shape[1])


def shards(
    dinv_root,
    rhs_root,
    dinv_mid,
    coup_mid,
    rhs_mid,
    dinv_leaf,
    coup_leaf,
    rhs_leaf,
    bounds_mid,
    bounds_leaf,
    parents,
):
    row_id = lax.axis_index("row")
    col_id = lax.axis_index("col")
    x, h, z, y = row_id // 2, row_id % 2, col_id // 2, col_id % 2
    place = jnp.stack([x, h, z, y]).astype(jnp.int32)
    rhs_width = rhs_root.shape[1]
    local = dinv_root.shape[0] // BLOCK
    slot = local // 8
    half = local // 2
    leaf_slots = bounds_leaf.shape[1] // 4
    at = plan_layout(local, slot, leaf_slots)

    order = pl.pallas_call(
        functools.partial(order_kernel, local, slot),
        out_shape=jax.ShapeDtypeStruct((local,), jnp.int32),
        in_specs=[SMEM] * 2,
        out_specs=SMEM,
        scratch_shapes=[pltpu.SMEM((4 * local,), jnp.int32)],
    )(place, bounds_mid)
    plan = pl.pallas_call(
        functools.partial(plan_kernel, local, slot, leaf_slots),
        out_shape=jax.ShapeDtypeStruct((at["size"],), jnp.int32),
        in_specs=[SMEM] * 4,
        out_specs=SMEM,
        scratch_shapes=[pltpu.SMEM((4 * local,), jnp.int32)] * 3,
    )(place, bounds_mid, bounds_leaf, parents)

    near = jnp.arange(local, dtype=jnp.int32)
    near_y, near_z, near_k = near // half, near % half // slot, near % slot
    mid_order = (2 * (z ^ near_z) + (y ^ near_y)) * slot + near_k
    leaf_order = jnp.stack(
        [2 * x + 1 - h, 2 * (1 - x) + 1 - h, 2 * x + h, 2 * (1 - x) + h]
    ).astype(jnp.int32)

    root_rhs = rhs_root.T
    mid_rhs = lax.dynamic_index_in_dim(rhs_mid, x, 0, keepdims=False).T
    leaf_rhs = rhs_leaf[0].T
    leaf_cols = coup_leaf.shape[2] // 4

    def chain(lo, hi):
        value = root_rhs[lo:hi]
        send = row_product(order, half, half, value, dinv_root)
        keep = row_product(order, 0, half, value, dinv_root)
        got = reduce_columns(send, keep, slot)
        picked = gather(plan, at["select"], slot, got, swap(got, "row", 1), swap(got, "row", 2))
        own = gather_columns(picked)
        sib = swap(own, "row", 1)
        asked = swap(gather(plan, at["send_root"], leaf_slots + slot, own, sib), "row", 2)
        root_out = natural(gather(plan, at["out"], slot, own, sib, asked))

        term = mid_coupling(plan, at["mid"], own, sib, coup_mid)
        shift = (mid_rhs[lo:hi] - (term + swap(term, "row", 1))).astype(BF16)
        send = row_product(mid_order, half, half, shift, dinv_mid)
        keep = row_product(mid_order, 0, half, shift, dinv_mid)
        got = reduce_columns(send, keep, slot)
        mid_out = natural(got)
        mid_own = gather_columns(got)
        mid_sib = swap(mid_own, "row", 1)
        mid_asked = swap(gather(plan, at["send_mid"], leaf_slots, mid_own, mid_sib), "row", 2)

        bound = gather(plan, at["leaf"], leaf_slots, own, sib, asked, mid_own, mid_sib, mid_asked)
        bound = jnp.swapaxes(bound, 0, 1).reshape(hi - lo, leaf_slots * BLOCK)

        def reduce_rows(send, keep):
            part = add(keep, swap(send, "row", 1))
            return add(part[0], swap(part[1].astype(BF16), "row", 2))

        term = reduce_rows(
            leaf_coupling(leaf_order, 0, 2, bound, coup_leaf[0], leaf_cols),
            leaf_coupling(leaf_order, 2, 2, bound, coup_leaf[0], leaf_cols),
        )
        shift = (leaf_rhs[lo:hi] - term).astype(BF16)
        leaf_out = reduce_rows(
            leaf_inverse(leaf_order, 0, 2, shift, dinv_leaf[0]),
            leaf_inverse(leaf_order, 2, 2, shift, dinv_leaf[0]),
        ).astype(BF16)
        return root_out, mid_out, leaf_out.T

    step = rhs_width // CHUNKS
    results = [chain(i * step, (i + 1) * step) for i in range(CHUNKS)]
    root_values, mid_values, leaf_values = (jnp.concatenate(part, axis=1) for part in zip(*results))
    return (root_values, mid_values, leaf_values[None])


def solution(mesh):
    sizes = dict(mesh.shape)
    in_specs = (
        P("row", "col"),
        P("col", None),
        P("row", "col"),
        P("row", "col"),
        P(None, "col", None),
        P("col", None, "row"),
        P("col", "row", None),
        P("col", "row", None),
        P(),
        P(),
        P(),
    )
    out_specs = (P(("row", "col"), None), P(("row", "col"), None), P("col", "row", None))

    def run(*args):
        fronts, listed = args[8].shape
        blocks = args[0].shape[0] // BLOCK
        whole = fronts == 2 and fronts * listed == blocks and args[2].shape[0] == args[0].shape[0]
        fits = sizes["row"] == 4 and sizes["col"] == 8 and whole
        body = shards if fits else general_shards
        return jax.shard_map(body, mesh=mesh, in_specs=in_specs, out_specs=out_specs, check_vma=False)(*args)

    return run
```

```python
import functools

import jax
import jax.numpy as jnp
from jax import lax
from jax.experimental import pallas as pl
from jax.experimental.pallas import tpu as pltpu
from jax.sharding import PartitionSpec as P

BLOCK = 128
F32 = jnp.float32
BF16 = jnp.bfloat16
NT = (((1,), (1,)), ((), ()))
NN = (((1,), (0,)), ((), ()))


def partner(value, axis, distance):
    mask = 2**distance
    pairs = [(source, source ^ mask) for source in range(lax.axis_size(axis))]
    return lax.ppermute(value, axis, pairs)


def pick_blocks(shard_rows, wanted):
    block_count = shard_rows.shape[0] // BLOCK
    flat_blocks = shard_rows.reshape(block_count, BLOCK * shard_rows.shape[1])
    present = jnp.arange(block_count, dtype=jnp.int32)
    select = (wanted[:, None] == present[None, :]).astype(shard_rows.dtype)
    return jnp.dot(select, flat_blocks, preferred_element_type=F32)


def transposed_product(coupling, boundary):
    return lax.dot_general(coupling, boundary, (((0,), (0,)), ((), ())), preferred_element_type=F32)


def general_shards(
    dinv_root,
    rhs_root,
    dinv_mid,
    coup_mid,
    rhs_mid,
    dinv_leaf,
    coup_leaf,
    rhs_leaf,
    bounds_mid,
    bounds_leaf,
    parents,
):
    row_total = lax.axis_size("row")
    row_id = lax.axis_index("row")
    col_id = lax.axis_index("col")
    rhs_width = rhs_root.shape[1]
    root_total = dinv_root.shape[0] * row_total // BLOCK
    front_mid = row_id // 2
    half_index = row_id % 2
    half_blocks = bounds_mid.shape[1] // 2
    mid_all = lax.dynamic_slice_in_dim(bounds_mid, front_mid, 1, 0)[0]
    mid_list = lax.dynamic_slice_in_dim(mid_all, half_index * half_blocks, half_blocks, 0)
    leaf_all = lax.dynamic_slice_in_dim(bounds_leaf, col_id, 1, 0)[0]
    leaf_slots = leaf_all.shape[0] // row_total
    leaf_list = lax.dynamic_slice_in_dim(leaf_all, row_id * leaf_slots, leaf_slots, 0)
    wanted = jnp.concatenate([mid_list, leaf_list])
    root_values = lax.psum_scatter(
        jnp.dot(dinv_root, rhs_root, preferred_element_type=F32),
        "col",
        scatter_dimension=0,
        tiled=True,
    ).astype(BF16)
    picked = pick_blocks(lax.all_gather(root_values, ("row", "col"), axis=0, tiled=True), wanted)
    bound_mid = picked[:half_blocks].reshape(half_blocks * BLOCK, rhs_width).astype(BF16)
    root_side = picked[half_blocks:]
    mid_part = transposed_product(coup_mid, bound_mid)
    mid_terms = mid_part + partner(mid_part, "row", 0)
    rhs_here = lax.dynamic_slice_in_dim(rhs_mid, front_mid, 1, 0)[0]
    shift_mid = (rhs_here - mid_terms).astype(BF16)
    mid_values = lax.psum_scatter(
        jnp.dot(dinv_mid, shift_mid, preferred_element_type=F32),
        "col",
        scatter_dimension=0,
        tiled=True,
    ).astype(BF16)
    half_rows = lax.all_gather(mid_values, "col", axis=0, tiled=True)
    half_count = half_rows.shape[0] // BLOCK
    half_flat = half_rows.reshape(half_count, BLOCK * rhs_width)
    local_ids = leaf_all - root_total - half_index * half_count
    owns_parent = lax.dynamic_slice_in_dim(parents, col_id, 1, 0)[0] == front_mid
    choose = (
        (local_ids[:, None] == jnp.arange(half_count, dtype=jnp.int32)[None, :]) & owns_parent
    ).astype(BF16)
    from_parent = lax.psum_scatter(
        jnp.dot(choose, half_flat, preferred_element_type=F32).astype(BF16),
        "row",
        scatter_dimension=0,
        tiled=True,
    ).astype(F32)
    bound_leaf = (root_side + from_parent).reshape(leaf_slots * BLOCK, rhs_width).astype(BF16)
    leaf_sum = lax.psum_scatter(
        transposed_product(coup_leaf[0], bound_leaf), "row", scatter_dimension=0, tiled=True
    )
    shift_leaf = (rhs_leaf[0] - leaf_sum).astype(BF16)
    leaf_values = lax.psum_scatter(
        jnp.dot(dinv_leaf[0], shift_leaf, preferred_element_type=F32),
        "row",
        scatter_dimension=0,
        tiled=True,
    ).astype(BF16)
    return (root_values, mid_values, leaf_values[None])


SMEM = pl.BlockSpec(memory_space=pltpu.SMEM)
VMEM = pl.BlockSpec(memory_space=pltpu.VMEM)
ANY = pl.BlockSpec(memory_space=pl.ANY)
LIMIT = 48 * 1024 * 1024
CHAINS = ((1, 2, 4), (2, 1, 4))


def params():
    return pltpu.CompilerParams(vmem_limit_bytes=LIMIT)


def cost(rows, depth, width):
    return pl.CostEstimate(flops=2 * rows * depth * width, bytes_accessed=2 * rows * depth, transcendentals=0)


def loop(count, body):
    def step(i, carry):
        body(i)
        return carry

    lax.fori_loop(0, count, step, 0)


def place_of(chip, col, bits, slot):
    far = chip ^ col
    high, mid, low = (((far & bit) != 0).astype(jnp.int32) for bit in bits)
    return (4 * high + 2 * mid + low) * slot


def chips_in_order(col, bits):
    return [col ^ sum(bit for bit, shift in zip(bits, (4, 2, 1)) if t & shift) for t in range(8)]


def mark_fronts(bounds_ref, front):
    def body(j):
        front[bounds_ref[0, j]] = 0
        front[bounds_ref[1, j]] = 1

    loop(bounds_ref.shape[1], body)


def order_kernel(local, slot, place_ref, bounds_ref, out_ref, front):
    row, col = place_ref[0], place_ref[1]
    first = row * local
    mark_fronts(bounds_ref, front)
    before = lax.fori_loop(0, first, lambda v, s: s + 1 - front[v], jnp.int32(0))
    zeros = lax.fori_loop(0, local, lambda i, s: s + 1 - front[first + i], jnp.int32(0))

    def body(i, carry):
        low, high = carry
        kind = front[first + i]
        rank = jnp.where(kind == 0, low, zeros + high)
        out_ref[place_of((before + rank) & 7, col, CHAINS[0], slot) + (rank >> 3)] = i
        return low + 1 - kind, high + kind

    lax.fori_loop(0, local, body, (jnp.int32(0), jnp.int32(0)))


def plan_layout(local, slot, leaf_slots):
    at = {}
    size = 0
    for name, count in (
        ("select", slot),
        ("mid", local),
        ("send_root", leaf_slots + slot),
        ("leaf", leaf_slots),
        ("out", slot),
        ("send_mid", leaf_slots),
    ):
        at[name] = size
        size += count
    at["size"] = size
    at["mid_base"] = 2 * local + leaf_slots + slot
    return at


def plan_kernel(local, slot, leaf_slots, place_ref, bounds_ref, leaf_ref, parents_ref, out_ref, front, ident, where):
    row, col = place_ref[0], place_ref[1]
    x, h = row // 2, row % 2
    total = 4 * local
    mark_fronts(bounds_ref, front)
    chains = range(len(CHAINS))
    at = plan_layout(local, slot, leaf_slots)

    def per_row(r, before):
        zeros = lax.fori_loop(0, local, lambda i, s: s + 1 - front[r * local + i], jnp.int32(0))

        def body(i, carry):
            low, high = carry
            kind = front[r * local + i]
            rank = jnp.where(kind == 0, low, zeros + high)
            chip = (before + rank) & 7
            ident[r * local + chip * slot + (rank >> 3)] = r * local + i
            return low + 1 - kind, high + kind

        lax.fori_loop(0, local, body, (jnp.int32(0), jnp.int32(0)))
        return before + zeros

    lax.fori_loop(0, 4, per_row, jnp.int32(0))

    def clear(v):
        for n in chains:
            where[n, v] = 0

    loop(total, clear)

    def per_chip(chip, _):
        here = chip == col
        near = [place_of(chip, col, bits, slot) for bits in CHAINS]

        def put(core, count, block, code):
            for n in chains:
                where[n, block] = (core ^ h) * local + near[n] + count

            @pl.when(here & (core == h))
            def _():
                for n in chains:
                    out_ref[n, count] = code

        def from_far(step, carry):
            count0, count1 = carry
            core, k = step // slot, step % slot
            block = ident[(2 * (1 - x) + core) * local + chip * slot + k]
            taken = front[block] == x
            count = jnp.where(core == 0, count0, count1)

            @pl.when(taken)
            def _():
                put(core, count, block, 2 * slot + k)

            add = taken.astype(jnp.int32)
            return count0 + jnp.where(core == 0, add, 0), count1 + jnp.where(core == 0, 0, add)

        counts = lax.fori_loop(0, 2 * slot, from_far, (jnp.int32(0), jnp.int32(0)))

        def from_near(step, carry):
            count0, count1 = carry
            owner, k = step // slot, step % slot
            block = ident[(2 * x + owner) * local + chip * slot + k]
            taken = front[block] == x
            core = (count0 >= slot).astype(jnp.int32)
            count = jnp.where(core == 0, count0, count1)

            @pl.when(taken)
            def _():
                put(core, count, block, (owner ^ core) * slot + k)

            add = taken.astype(jnp.int32)
            return count0 + jnp.where(core == 0, add, 0), count1 + jnp.where(core == 0, 0, add)

        lax.fori_loop(0, 2 * slot, from_near, counts)
        return 0

    lax.fori_loop(0, 8, per_chip, 0)

    def mid_place(block, bits):
        inner = block % local
        return ((block // local) ^ h) * local + place_of(inner // slot, col, bits, slot) + inner % slot

    def mid_list(j):
        block = bounds_ref[x, h * local + j]
        for n in chains:
            out_ref[n, at["mid"] + j] = where[n, block]

    loop(local, mid_list)
    far = 2 * (1 - x) + h
    owner = parents_ref[col] == x

    def lists(j):
        asked = leaf_ref[col, far * leaf_slots + j]
        held = leaf_ref[col, row * leaf_slots + j]
        low = jnp.minimum(held, total - 1)
        for n in chains:
            bits = CHAINS[n]
            out_ref[n, at["send_root"] + j] = where[n, jnp.minimum(asked, total - 1)]
            out_ref[n, at["send_mid"] + j] = mid_place(jnp.maximum(asked - total, 0), bits)
            from_root = jnp.where(front[low] == x, where[n, low], 2 * local + j)
            from_mid = jnp.where(owner, mid_place(jnp.maximum(held - total, 0), bits), 2 * local + j)
            out_ref[n, at["leaf"] + j] = jnp.where(held < total, from_root, from_mid + at["mid_base"])

    loop(leaf_slots, lists)

    def outs(j):
        asked = far * local + col * slot + j
        held = row * local + col * slot + j
        for n in chains:
            out_ref[n, at["send_root"] + leaf_slots + j] = where[n, asked]
            out_ref[n, at["out"] + j] = jnp.where(front[held] == x, where[n, held], 2 * local + leaf_slots + j)

    loop(slot, outs)


def start_fetch(sources, code, target, sem):
    base = 0
    for source in sources:
        count = source.shape[0]

        @pl.when((code >= base) & (code < base + count))
        def _(source=source, base=base):
            pltpu.make_async_copy(source.at[code - base], target, sem).start()

        base += count


def lanes(ref, i):
    return ref.at[:, pl.ds(i * BLOCK, BLOCK)]


def gather_kernel(chain, start, count, wide, table_ref, *refs):
    *sources, out_ref, sems = refs
    targets = [lanes(out_ref, i) if wide else out_ref.at[i] for i in range(count)]
    for i in range(count):
        start_fetch(sources, table_ref[chain, start + i], targets[i], sems.at[i])
    for i in range(count):
        pltpu.make_async_copy(sources[0].at[0], targets[i], sems.at[i]).wait()


def gather(table, chain, start, count, *sources, wide=False):
    width = sources[0].shape[1]
    shape = (width, count * BLOCK) if wide else (count, width, BLOCK)
    return pl.pallas_call(
        functools.partial(gather_kernel, chain, start, count, wide),
        out_shape=jax.ShapeDtypeStruct(shape, BF16),
        in_specs=[SMEM] + [ANY] * len(sources),
        out_specs=VMEM,
        scratch_shapes=[pltpu.SemaphoreType.DMA((count,))],
        compiler_params=params(),
    )(table, *sources)


def root_product_kernel(parts, order_ref, value_ref, *refs):
    blocks, outs = refs[:parts], refs[parts:]
    step = pl.program_id(0)
    matrix = jnp.concatenate([b[...] for b in blocks], axis=0)
    result = lax.dot_general(value_ref[...], matrix, NT, preferred_element_type=F32)
    width = result.shape[0] // 2
    for n, bit in enumerate((2, 1)):
        part = result[n * width : (n + 1) * width]

        def store(ref, part=part):
            for i in range(parts):
                ref[i] = part[:, i * BLOCK : (i + 1) * BLOCK].astype(ref.dtype)

        far = (3 - step) & bit

        @pl.when(far != 0)
        def _(n=n, store=store):
            store(outs[2 * n])

        @pl.when(far == 0)
        def _(n=n, store=store):
            store(outs[2 * n + 1])


def root_product(order, value, matrix):
    width, depth = value.shape
    local = matrix.shape[0] // BLOCK
    parts = local // 4

    def spec(i):
        return pl.BlockSpec((BLOCK, depth), lambda s, order: (order[parts * (3 - s) + i], 0))

    out_specs, out_shape = [], []
    for bit in (2, 1):
        for far in (True, False):
            seen = [s for s in range(4) if bool((3 - s) & bit) == far]
            index = [1 - min(sum(1 for t in seen if t < s), 1) for s in range(4)]

            def block(s, order, index=index):
                picked = functools.reduce(lambda acc, t: jnp.where(s == t, index[t], acc), range(1, 4), index[0])
                return (picked, 0, 0)

            out_specs.append(pl.BlockSpec((parts, width // 2, BLOCK), block))
            out_shape.append(jax.ShapeDtypeStruct((local // 2, width // 2, BLOCK), BF16 if far else F32))
    outs = pl.pallas_call(
        functools.partial(root_product_kernel, parts),
        grid_spec=pltpu.PrefetchScalarGridSpec(
            num_scalar_prefetch=1,
            grid=(4,),
            in_specs=[pl.BlockSpec((width, depth), lambda s, order: (0, 0))] + [spec(i) for i in range(parts)],
            out_specs=out_specs,
        ),
        out_shape=out_shape,
        compiler_params=params(),
        cost_estimate=cost(matrix.shape[0], depth, width),
    )(order, value, *([matrix] * parts))
    return outs[:2], outs[2:]


def mid_product_kernel(parts, order_ref, value_ref, *refs):
    blocks, (send_ref, keep_ref) = refs[:parts], refs[parts:]
    step = pl.program_id(0)
    matrix = jnp.concatenate([b[...] for b in blocks], axis=0)
    result = lax.dot_general(value_ref[...], matrix, NT, preferred_element_type=F32)

    def store(ref):
        for i in range(parts):
            ref[i] = result[:, i * BLOCK : (i + 1) * BLOCK].astype(ref.dtype)

    @pl.when(step < 2)
    def _():
        store(send_ref)

    @pl.when(step >= 2)
    def _():
        store(keep_ref)


def mid_product(order, value, matrix):
    width, depth = value.shape
    local = matrix.shape[0] // BLOCK
    parts = local // 4

    def spec(i):
        return pl.BlockSpec((BLOCK, depth), lambda s, order: (order[parts * ((s + 2) % 4) + i], 0))

    return pl.pallas_call(
        functools.partial(mid_product_kernel, parts),
        grid_spec=pltpu.PrefetchScalarGridSpec(
            num_scalar_prefetch=1,
            grid=(4,),
            in_specs=[pl.BlockSpec((width, depth), lambda s, order: (0, 0))] + [spec(i) for i in range(parts)],
            out_specs=[
                pl.BlockSpec((parts, width, BLOCK), lambda s, order: (jnp.minimum(s, 1), 0, 0)),
                pl.BlockSpec((parts, width, BLOCK), lambda s, order: (jnp.maximum(s - 2, 0), 0, 0)),
            ],
        ),
        out_shape=[
            jax.ShapeDtypeStruct((local // 2, width, BLOCK), BF16),
            jax.ShapeDtypeStruct((local // 2, width, BLOCK), F32),
        ],
        compiler_params=params(),
        cost_estimate=cost(matrix.shape[0], depth, width),
    )(order, value, *([matrix] * parts))


def mid_coupling_kernel(value_ref, coup_ref, out_ref):
    out_ref[...] = lax.dot_general(value_ref[...], coup_ref[...], NN, preferred_element_type=F32)


def mid_coupling(value, coup, steps=4):
    width, depth = value.shape
    cols = coup.shape[1]
    return pl.pallas_call(
        mid_coupling_kernel,
        grid=(steps,),
        in_specs=[
            pl.BlockSpec((width, depth), lambda s: (0, 0)),
            pl.BlockSpec((depth, cols // steps), lambda s: (0, s)),
        ],
        out_specs=pl.BlockSpec((width, cols // steps), lambda s: (0, s)),
        out_shape=jax.ShapeDtypeStruct((width, cols), F32),
        compiler_params=params(),
        cost_estimate=cost(cols, depth, width),
    )(value, coup)


def leaf_kernel(dims, order_ref, value_ref, matrix_ref, out_ref):
    product = lax.dot_general(value_ref[...], matrix_ref[...], dims, preferred_element_type=F32)
    out_ref[0] = product.astype(out_ref.dtype)


def leaf_product(order, start, dims, value, matrix, cols, kind):
    width, depth = value.shape
    if dims is NN:
        spec = pl.BlockSpec((depth, cols), lambda s, order: (0, order[start + s]))
    else:
        spec = pl.BlockSpec((cols, depth), lambda s, order: (order[start + s], 0))
    return pl.pallas_call(
        functools.partial(leaf_kernel, dims),
        grid_spec=pltpu.PrefetchScalarGridSpec(
            num_scalar_prefetch=1,
            grid=(2,),
            in_specs=[pl.BlockSpec((width, depth), lambda s, order: (0, 0)), spec],
            out_specs=pl.BlockSpec((1, width, cols), lambda s, order: (s, 0, 0)),
        ),
        out_shape=jax.ShapeDtypeStruct((2, width, cols), kind),
        compiler_params=params(),
        cost_estimate=cost(2 * cols, depth, width),
    )(order, value, matrix)


def swap(value, axis, mask):
    return lax.ppermute(value, axis, [(i, i ^ mask) for i in range(lax.axis_size(axis))])


def add(*terms):
    return functools.reduce(jnp.add, [t.astype(F32) for t in terms])


def reduce_columns(send, keep, bits):
    got = swap(send, "col", bits[0])
    for bit in bits[1:]:
        half = got.shape[0] // 2
        send = add(keep[half:], got[half:]).astype(BF16)
        keep = add(keep[:half], got[:half])
        got = swap(send, "col", bit)
    return add(keep, got).astype(BF16)


def gather_columns(value, bits):
    for bit in reversed(bits):
        value = jnp.concatenate([value, swap(value, "col", bit)], axis=0)
    return value


def natural(parts):
    blocks = jnp.concatenate(parts, axis=1)
    return jnp.swapaxes(blocks, 1, 2).reshape(-1, blocks.shape[1])


def shards(
    dinv_root,
    rhs_root,
    dinv_mid,
    coup_mid,
    rhs_mid,
    dinv_leaf,
    coup_leaf,
    rhs_leaf,
    bounds_mid,
    bounds_leaf,
    parents,
):
    row_id = lax.axis_index("row")
    col_id = lax.axis_index("col")
    x, h = row_id // 2, row_id % 2
    place = jnp.stack([row_id, col_id]).astype(jnp.int32)
    local = dinv_root.shape[0] // BLOCK
    slot = local // 8
    leaf_slots = bounds_leaf.shape[1] // 4
    at = plan_layout(local, slot, leaf_slots)
    chains = range(len(CHAINS))

    order = pl.pallas_call(
        functools.partial(order_kernel, local, slot),
        out_shape=jax.ShapeDtypeStruct((local,), jnp.int32),
        in_specs=[SMEM] * 2,
        out_specs=SMEM,
        scratch_shapes=[pltpu.SMEM((4 * local,), jnp.int32)],
    )(place, bounds_mid)
    plan = pl.pallas_call(
        functools.partial(plan_kernel, local, slot, leaf_slots),
        out_shape=jax.ShapeDtypeStruct((len(CHAINS), at["size"]), jnp.int32),
        in_specs=[SMEM] * 4,
        out_specs=SMEM,
        scratch_shapes=[pltpu.SMEM((4 * local,), jnp.int32)] * 2
        + [pltpu.SMEM((len(CHAINS), 4 * local), jnp.int32)],
    )(place, bounds_mid, bounds_leaf, parents)

    within = jnp.arange(slot, dtype=jnp.int32)
    leaf_order = jnp.stack([2 * x + 1 - h, 2 * (1 - x) + 1 - h, 2 * x + h, 2 * (1 - x) + h]).astype(jnp.int32)
    mid_rhs = lax.dynamic_index_in_dim(rhs_mid, x, 0, keepdims=False).T
    leaf_rhs = rhs_leaf[0].T
    leaf_cols = coup_leaf.shape[2] // 4
    sent = root_product(order, rhs_root.T, dinv_root)

    def reduce_rows(dims, value, matrix):
        send = leaf_product(leaf_order, 0, dims, value, matrix, leaf_cols, BF16)
        keep = leaf_product(leaf_order, 2, dims, value, matrix, leaf_cols, F32)
        got = swap(send, "row", 1)
        far = swap(add(keep[1], got[1]).astype(BF16), "row", 2)
        return add(keep[0], got[0], far)

    def chain(n):
        bits = CHAINS[n]
        got = reduce_columns(*sent[n], bits)
        picked = gather(plan, n, at["select"], slot, got, swap(got, "row", 1), swap(got, "row", 2))
        own = gather_columns(picked, bits)
        sib = swap(own, "row", 1)
        bound = gather(plan, n, at["mid"], local, own, sib, wide=True)
        asked = swap(gather(plan, n, at["send_root"], leaf_slots + slot, own, sib), "row", 2)
        root_out = gather(plan, n, at["out"], slot, own, sib, asked)

        term = mid_coupling(bound, coup_mid)
        width = term.shape[0]
        rhs = mid_rhs[n * width : (n + 1) * width]
        shift = (rhs - (term + swap(term, "row", 1))).astype(BF16)
        mid_order = jnp.concatenate([chip * slot + within for chip in chips_in_order(col_id, bits)])
        mid_out = reduce_columns(*mid_product(mid_order.astype(jnp.int32), shift, dinv_mid), bits)
        mid_own = gather_columns(mid_out, bits)
        mid_sib = swap(mid_own, "row", 1)
        mid_asked = swap(gather(plan, n, at["send_mid"], leaf_slots, mid_own, mid_sib), "row", 2)

        sources = (own, sib, asked, mid_own, mid_sib, mid_asked)
        bound = gather(plan, n, at["leaf"], leaf_slots, *sources, wide=True)
        rhs = leaf_rhs[n * width : (n + 1) * width]
        shift = (rhs - reduce_rows(NN, bound, coup_leaf[0])).astype(BF16)
        leaf_out = reduce_rows(NT, shift, dinv_leaf[0]).astype(BF16)
        return root_out, mid_out, leaf_out

    root_values, mid_values, leaf_values = zip(*[chain(n) for n in chains])
    return (natural(root_values), natural(mid_values), jnp.concatenate(leaf_values, axis=0).T[None])


def solution(mesh):
    sizes = dict(mesh.shape)
    in_specs = (
        P("row", "col"),
        P("col", None),
        P("row", "col"),
        P("row", "col"),
        P(None, "col", None),
        P("col", None, "row"),
        P("col", "row", None),
        P("col", "row", None),
        P(),
        P(),
        P(),
    )
    out_specs = (P(("row", "col"), None), P(("row", "col"), None), P("col", "row", None))

    def run(*args):
        fronts, listed = args[8].shape
        blocks = args[0].shape[0] // BLOCK
        whole = fronts == 2 and fronts * listed == blocks and args[2].shape[0] == args[0].shape[0]
        fits = sizes["row"] == 4 and sizes["col"] == 8 and whole
        body = shards if fits else general_shards
        return jax.shard_map(body, mesh=mesh, in_specs=in_specs, out_specs=out_specs, check_vma=False)(*args)

    return run
```

```python
import functools

import jax
import jax.numpy as jnp
from jax import lax
from jax.experimental import pallas as pl
from jax.experimental.pallas import tpu as pltpu
from jax.sharding import PartitionSpec as P

BLOCK = 128
F32 = jnp.float32
BF16 = jnp.bfloat16
NT = (((1,), (1,)), ((), ()))
NN = (((1,), (0,)), ((), ()))


def partner(value, axis, distance):
    mask = 2**distance
    pairs = [(source, source ^ mask) for source in range(lax.axis_size(axis))]
    return lax.ppermute(value, axis, pairs)


def pick_blocks(shard_rows, wanted):
    block_count = shard_rows.shape[0] // BLOCK
    flat_blocks = shard_rows.reshape(block_count, BLOCK * shard_rows.shape[1])
    present = jnp.arange(block_count, dtype=jnp.int32)
    select = (wanted[:, None] == present[None, :]).astype(shard_rows.dtype)
    return jnp.dot(select, flat_blocks, preferred_element_type=F32)


def transposed_product(coupling, boundary):
    return lax.dot_general(coupling, boundary, (((0,), (0,)), ((), ())), preferred_element_type=F32)


def general_shards(
    dinv_root,
    rhs_root,
    dinv_mid,
    coup_mid,
    rhs_mid,
    dinv_leaf,
    coup_leaf,
    rhs_leaf,
    bounds_mid,
    bounds_leaf,
    parents,
):
    row_total = lax.axis_size("row")
    row_id = lax.axis_index("row")
    col_id = lax.axis_index("col")
    rhs_width = rhs_root.shape[1]
    root_total = dinv_root.shape[0] * row_total // BLOCK
    front_mid = row_id // 2
    half_index = row_id % 2
    half_blocks = bounds_mid.shape[1] // 2
    mid_all = lax.dynamic_slice_in_dim(bounds_mid, front_mid, 1, 0)[0]
    mid_list = lax.dynamic_slice_in_dim(mid_all, half_index * half_blocks, half_blocks, 0)
    leaf_all = lax.dynamic_slice_in_dim(bounds_leaf, col_id, 1, 0)[0]
    leaf_slots = leaf_all.shape[0] // row_total
    leaf_list = lax.dynamic_slice_in_dim(leaf_all, row_id * leaf_slots, leaf_slots, 0)
    wanted = jnp.concatenate([mid_list, leaf_list])
    root_values = lax.psum_scatter(
        jnp.dot(dinv_root, rhs_root, preferred_element_type=F32),
        "col",
        scatter_dimension=0,
        tiled=True,
    ).astype(BF16)
    picked = pick_blocks(lax.all_gather(root_values, ("row", "col"), axis=0, tiled=True), wanted)
    bound_mid = picked[:half_blocks].reshape(half_blocks * BLOCK, rhs_width).astype(BF16)
    root_side = picked[half_blocks:]
    mid_part = transposed_product(coup_mid, bound_mid)
    mid_terms = mid_part + partner(mid_part, "row", 0)
    rhs_here = lax.dynamic_slice_in_dim(rhs_mid, front_mid, 1, 0)[0]
    shift_mid = (rhs_here - mid_terms).astype(BF16)
    mid_values = lax.psum_scatter(
        jnp.dot(dinv_mid, shift_mid, preferred_element_type=F32),
        "col",
        scatter_dimension=0,
        tiled=True,
    ).astype(BF16)
    half_rows = lax.all_gather(mid_values, "col", axis=0, tiled=True)
    half_count = half_rows.shape[0] // BLOCK
    half_flat = half_rows.reshape(half_count, BLOCK * rhs_width)
    local_ids = leaf_all - root_total - half_index * half_count
    owns_parent = lax.dynamic_slice_in_dim(parents, col_id, 1, 0)[0] == front_mid
    choose = (
        (local_ids[:, None] == jnp.arange(half_count, dtype=jnp.int32)[None, :]) & owns_parent
    ).astype(BF16)
    from_parent = lax.psum_scatter(
        jnp.dot(choose, half_flat, preferred_element_type=F32).astype(BF16),
        "row",
        scatter_dimension=0,
        tiled=True,
    ).astype(F32)
    bound_leaf = (root_side + from_parent).reshape(leaf_slots * BLOCK, rhs_width).astype(BF16)
    leaf_sum = lax.psum_scatter(
        transposed_product(coup_leaf[0], bound_leaf), "row", scatter_dimension=0, tiled=True
    )
    shift_leaf = (rhs_leaf[0] - leaf_sum).astype(BF16)
    leaf_values = lax.psum_scatter(
        jnp.dot(dinv_leaf[0], shift_leaf, preferred_element_type=F32),
        "row",
        scatter_dimension=0,
        tiled=True,
    ).astype(BF16)
    return (root_values, mid_values, leaf_values[None])


SMEM = pl.BlockSpec(memory_space=pltpu.SMEM)
VMEM = pl.BlockSpec(memory_space=pltpu.VMEM)
ANY = pl.BlockSpec(memory_space=pl.ANY)
LIMIT = 48 * 1024 * 1024
CHAINS = ((1, 2, 4), (2, 1, 4))


def params():
    return pltpu.CompilerParams(vmem_limit_bytes=LIMIT)


def cost(rows, depth, width):
    return pl.CostEstimate(flops=2 * rows * depth * width, bytes_accessed=2 * rows * depth, transcendentals=0)


def loop(count, body):
    def step(i, carry):
        body(i)
        return carry

    lax.fori_loop(0, count, step, 0)


def place_of(chip, col, bits, slot):
    far = chip ^ col
    high, mid, low = (((far & bit) != 0).astype(jnp.int32) for bit in bits)
    return (4 * high + 2 * mid + low) * slot


def chips_in_order(col, bits):
    return [col ^ sum(bit for bit, shift in zip(bits, (4, 2, 1)) if t & shift) for t in range(8)]


def mark_fronts(bounds_ref, front):
    def body(j):
        front[bounds_ref[0, j]] = 0
        front[bounds_ref[1, j]] = 1

    loop(bounds_ref.shape[1], body)


def order_kernel(local, slot, place_ref, bounds_ref, out_ref, front):
    row, col = place_ref[0], place_ref[1]
    first = row * local
    mark_fronts(bounds_ref, front)
    before = lax.fori_loop(0, first, lambda v, s: s + 1 - front[v], jnp.int32(0))
    zeros = lax.fori_loop(0, local, lambda i, s: s + 1 - front[first + i], jnp.int32(0))

    def body(i, carry):
        low, high = carry
        kind = front[first + i]
        rank = jnp.where(kind == 0, low, zeros + high)
        out_ref[place_of((before + rank) & 7, col, CHAINS[0], slot) + (rank >> 3)] = i
        return low + 1 - kind, high + kind

    lax.fori_loop(0, local, body, (jnp.int32(0), jnp.int32(0)))


def plan_layout(local, slot, leaf_slots):
    at = {}
    size = 0
    for name, count in (
        ("select", slot),
        ("mid", local),
        ("send_root", leaf_slots + slot),
        ("leaf", leaf_slots),
        ("out", slot),
        ("mid_order", local),
        ("mid_out", slot),
        ("turn", 1),
    ):
        at[name] = size
        size += count
    at["size"] = size
    return at


def plan_kernel(local, slot, leaf_slots, place_ref, bounds_ref, leaf_ref, parents_ref, out_ref, front, ident, where, record):
    row, col = place_ref[0], place_ref[1]
    x, h = row // 2, row % 2
    total = 4 * local
    mark_fronts(bounds_ref, front)
    chains = range(len(CHAINS))
    at = plan_layout(local, slot, leaf_slots)

    def per_row(r, before):
        zeros = lax.fori_loop(0, local, lambda i, s: s + 1 - front[r * local + i], jnp.int32(0))

        def body(i, carry):
            low, high = carry
            kind = front[r * local + i]
            rank = jnp.where(kind == 0, low, zeros + high)
            chip = (before + rank) & 7
            ident[r * local + chip * slot + (rank >> 3)] = r * local + i
            return low + 1 - kind, high + kind

        lax.fori_loop(0, local, body, (jnp.int32(0), jnp.int32(0)))
        return before + zeros

    lax.fori_loop(0, 4, per_row, jnp.int32(0))

    def clear(v):
        for n in chains:
            where[n, v] = 0

    loop(total, clear)

    def per_chip(chip, _):
        here = chip == col
        near = [place_of(chip, col, bits, slot) for bits in CHAINS]

        def put(core, count, block, code):
            for n in chains:
                where[n, block] = (core ^ h) * local + near[n] + count

            @pl.when(here & (core == h))
            def _():
                for n in chains:
                    out_ref[n, count] = code

        def from_far(step, carry):
            count0, count1 = carry
            core, k = step // slot, step % slot
            block = ident[(2 * (1 - x) + core) * local + chip * slot + k]
            taken = front[block] == x
            count = jnp.where(core == 0, count0, count1)

            @pl.when(taken)
            def _():
                put(core, count, block, 2 * slot + k)

            add = taken.astype(jnp.int32)
            return count0 + jnp.where(core == 0, add, 0), count1 + jnp.where(core == 0, 0, add)

        counts = lax.fori_loop(0, 2 * slot, from_far, (jnp.int32(0), jnp.int32(0)))

        def from_near(step, carry):
            count0, count1 = carry
            owner, k = step // slot, step % slot
            block = ident[(2 * x + owner) * local + chip * slot + k]
            taken = front[block] == x
            core = (count0 >= slot).astype(jnp.int32)
            count = jnp.where(core == 0, count0, count1)

            @pl.when(taken)
            def _():
                put(core, count, block, (owner ^ core) * slot + k)

            add = taken.astype(jnp.int32)
            return count0 + jnp.where(core == 0, add, 0), count1 + jnp.where(core == 0, 0, add)

        lax.fori_loop(0, 2 * slot, from_near, counts)
        return 0

    lax.fori_loop(0, 8, per_chip, 0)

    def mid_list(j):
        block = bounds_ref[x, h * local + j]
        for n in chains:
            out_ref[n, at["mid"] + j] = where[n, block]

    loop(local, mid_list)
    far = 2 * (1 - x) + h
    turn = jnp.int32(6)
    for k in range(7, 0, -1):
        apart = [(parents_ref[c] != parents_ref[c ^ k]).astype(jnp.int32) for c in range(8)]
        turn = jnp.where(functools.reduce(jnp.multiply, apart) == 1, k - 1, turn)
    out_ref[0, at["turn"]] = turn
    listed = 4 * leaf_slots

    def per_leaf(leaf, _):
        @pl.when(parents_ref[leaf] == x)
        def _():
            def body(j, rank):
                block = leaf_ref[leaf, j]
                taken = block >= total

                @pl.when(taken)
                def _():
                    record[block - total] = leaf * 4 * slot + rank

                return rank + taken.astype(jnp.int32)

            lax.fori_loop(0, listed, body, jnp.int32(0))

        return 0

    lax.fori_loop(0, 8, per_leaf, 0)

    def spot(block):
        leaf, rank = record[block] // (4 * slot), record[block] % (4 * slot)
        chip = jnp.where(rank < 2 * slot, leaf, leaf ^ (turn + 1))
        return chip, rank // slot % 2, rank % slot

    def mid_orders(block):
        chip, core, k = spot(block)

        @pl.when(core == h)
        def _():
            for n in chains:
                near = place_of(chip, col, CHAINS[n], slot) + k
                out_ref[n, at["mid_order"] + near] = (block // local ^ h) * local + block % local

    loop(2 * local, mid_orders)

    def mid_outs(j):
        chip, core, k = spot(h * local + col * slot + j)
        for n in chains:
            out_ref[n, at["mid_out"] + j] = (core ^ h) * local + place_of(chip, col, CHAINS[n], slot) + k

    loop(slot, mid_outs)

    def sends(j):
        asked = leaf_ref[col, far * leaf_slots + j]
        for n in chains:
            out_ref[n, at["send_root"] + j] = where[n, jnp.minimum(asked, total - 1)]

    loop(leaf_slots, sends)

    def count(j, rank):
        return rank + (leaf_ref[col, j] >= total).astype(jnp.int32)

    def lists(j, rank):
        held = leaf_ref[col, row * leaf_slots + j]
        low = jnp.minimum(held, total - 1)
        near = (rank // slot % 2 ^ h) * 2 * slot + rank // (2 * slot) * slot + rank % slot
        for n in chains:
            from_root = jnp.where(front[low] == x, where[n, low], 2 * local + j)
            from_mid = 2 * local + leaf_slots + slot + near
            out_ref[n, at["leaf"] + j] = jnp.where(held < total, from_root, from_mid)
        return count(row * leaf_slots + j, rank)

    lax.fori_loop(0, leaf_slots, lists, lax.fori_loop(0, row * leaf_slots, count, jnp.int32(0)))

    def outs(j):
        asked = far * local + col * slot + j
        held = row * local + col * slot + j
        for n in chains:
            out_ref[n, at["send_root"] + leaf_slots + j] = where[n, asked]
            out_ref[n, at["out"] + j] = jnp.where(front[held] == x, where[n, held], 2 * local + leaf_slots + j)

    loop(slot, outs)


def start_fetch(sources, code, target, sem, rows=None):
    base = 0
    for source in sources:
        count = source.shape[0]

        @pl.when((code >= base) & (code < base + count))
        def _(source=source, base=base):
            block = source.at[code - base] if rows is None else source.at[code - base, rows]
            pltpu.make_async_copy(block, target, sem).start()

        base += count


def gather_kernel(chain, start, count, total, rows, table_ref, *refs):
    sources, out_ref, sems = refs[:total], refs[-2], refs[-1]
    for i in range(count):
        start_fetch(sources, table_ref[chain, start + i], out_ref.at[i], sems.at[i], rows)
    for i in range(count):
        pltpu.make_async_copy(sources[0].at[0, rows], out_ref.at[i], sems.at[i]).wait()


def gather(table, chain, start, count, sources, after=(), part=None):
    first, width = (0, sources[0].shape[1]) if part is None else part
    return pl.pallas_call(
        functools.partial(gather_kernel, chain, start, count, len(sources), pl.ds(first, width)),
        out_shape=jax.ShapeDtypeStruct((count, width, BLOCK), BF16),
        in_specs=[SMEM] + [ANY] * (len(sources) + len(after)),
        out_specs=VMEM,
        scratch_shapes=[pltpu.SemaphoreType.DMA((count,))],
        compiler_params=params(),
    )(table, *sources, *after)


def store_halves(step, result, parts, outs):
    width = result.shape[0] // 2
    for n, bit in enumerate((2, 1)):
        part = result[n * width : (n + 1) * width]

        def store(ref, part=part):
            for i in range(parts):
                ref[i] = part[:, i * BLOCK : (i + 1) * BLOCK].astype(ref.dtype)

        far = (3 - step) & bit

        @pl.when(far != 0)
        def _(n=n, store=store):
            store(outs[2 * n])

        @pl.when(far == 0)
        def _(n=n, store=store):
            store(outs[2 * n + 1])


def half_specs(local, parts, width):
    out_specs, out_shape = [], []
    for bit in (2, 1):
        for far in (True, False):
            seen = [s for s in range(4) if bool((3 - s) & bit) == far]
            index = [1 - min(sum(1 for t in seen if t < s), 1) for s in range(4)]

            def block(s, order, index=index):
                picked = functools.reduce(lambda acc, t: jnp.where(s == t, index[t], acc), range(1, 4), index[0])
                return (picked, 0, 0)

            out_specs.append(pl.BlockSpec((parts, width // 2, BLOCK), block))
            out_shape.append(jax.ShapeDtypeStruct((local // 2, width // 2, BLOCK), BF16 if far else F32))
    return out_specs, out_shape


def root_product_kernel(parts, order_ref, value_ref, *refs):
    blocks, outs, turned = refs[:parts], refs[parts:-1], refs[-1]
    step = pl.program_id(0)

    @pl.when(step == 0)
    def _():
        turned[...] = value_ref[...].T

    matrix = jnp.concatenate([b[...] for b in blocks], axis=0)
    result = lax.dot_general(turned[...], matrix, NT, preferred_element_type=F32)
    store_halves(step, result, parts, outs)


def root_product(order, value, matrix):
    depth, width = value.shape
    local = matrix.shape[0] // BLOCK
    parts = local // 4

    def spec(i):
        return pl.BlockSpec((BLOCK, depth), lambda s, order: (order[parts * (3 - s) + i], 0))

    out_specs, out_shape = half_specs(local, parts, width)
    outs = pl.pallas_call(
        functools.partial(root_product_kernel, parts),
        grid_spec=pltpu.PrefetchScalarGridSpec(
            num_scalar_prefetch=1,
            grid=(4,),
            in_specs=[pl.BlockSpec((depth, width), lambda s, order: (0, 0))] + [spec(i) for i in range(parts)],
            out_specs=out_specs,
            scratch_shapes=[pltpu.VMEM((width, depth), BF16)],
        ),
        out_shape=out_shape,
        compiler_params=params(),
        cost_estimate=cost(matrix.shape[0], depth, width),
    )(order, value, *([matrix] * parts))
    return outs[:2], outs[2:]


def store_blocks(ref, result):
    for i in range(ref.shape[0]):
        ref[i] = result[:, i * BLOCK : (i + 1) * BLOCK].astype(ref.dtype)


def mid_first_kernel(front_ref, term_ref, got_ref, rhs_ref, matrix_ref, out_ref, shift_ref):
    @pl.when(pl.program_id(0) == 0)
    def _():
        shift_ref[...] = (rhs_ref[0].T.astype(F32) - (term_ref[...] + got_ref[...].astype(F32))).astype(BF16)

    store_blocks(out_ref, lax.dot_general(shift_ref[...], matrix_ref[...], NT, preferred_element_type=F32))


def mid_rest_kernel(shift_ref, matrix_ref, out_ref):
    store_blocks(out_ref, lax.dot_general(shift_ref[...], matrix_ref[...], NT, preferred_element_type=F32))


def mid_first(front, term, got, rhs, matrix):
    width, depth = term.shape
    half = matrix.shape[0] // BLOCK // 2
    whole = pl.BlockSpec((width, depth), lambda s, front: (0, 0))
    return pl.pallas_call(
        mid_first_kernel,
        grid_spec=pltpu.PrefetchScalarGridSpec(
            num_scalar_prefetch=1,
            grid=(2,),
            in_specs=[
                whole,
                whole,
                pl.BlockSpec((1, depth, width), lambda s, front: (front[0], 0, 0)),
                pl.BlockSpec((half // 2 * BLOCK, depth), lambda s, front: (s, 0)),
            ],
            out_specs=[pl.BlockSpec((half // 2, width, BLOCK), lambda s, front: (s, 0, 0)), whole],
        ),
        out_shape=[
            jax.ShapeDtypeStruct((half, width, BLOCK), BF16),
            jax.ShapeDtypeStruct((width, depth), BF16),
        ],
        compiler_params=params(),
        cost_estimate=cost(half * BLOCK, depth, width),
    )(front.reshape(1), term, got, rhs, matrix)


def mid_rest(shift, matrix):
    width, depth = shift.shape
    half = matrix.shape[0] // BLOCK // 2
    return pl.pallas_call(
        mid_rest_kernel,
        grid=(2,),
        in_specs=[
            pl.BlockSpec((width, depth), lambda s: (0, 0)),
            pl.BlockSpec((half // 2 * BLOCK, depth), lambda s: (2 + s, 0)),
        ],
        out_specs=pl.BlockSpec((half // 2, width, BLOCK), lambda s: (s, 0, 0)),
        out_shape=jax.ShapeDtypeStruct((half, width, BLOCK), BF16),
        compiler_params=params(),
        cost_estimate=cost(half * BLOCK, depth, width),
    )(shift, matrix)


def mid_coupling_kernel(start, count, table_ref, *refs):
    sources, (coup_ref, out_ref, send_ref, bound, sems) = refs[:4], refs[4:]
    width = bound.shape[0] // 2

    def target(n, i):
        return bound.at[pl.ds(n * width, width), pl.ds(i * BLOCK, BLOCK)]

    @pl.when(pl.program_id(0) == 0)
    def _():
        for n in range(2):
            for i in range(count):
                start_fetch(sources[2 * n : 2 * n + 2], table_ref[n, start + i], target(n, i), sems.at[n, i])
        for n in range(2):
            for i in range(count):
                pltpu.make_async_copy(sources[0].at[0], target(n, i), sems.at[n, i]).wait()

    product = lax.dot_general(bound[...], coup_ref[...], NN, preferred_element_type=F32)
    out_ref[...] = product
    send_ref[...] = product.astype(BF16)


def mid_coupling(table, start, sources, coup, steps=4):
    count, width, _ = sources[0].shape
    depth, cols = coup.shape
    tile = pl.BlockSpec((2 * width, cols // steps), lambda s: (0, s))
    return pl.pallas_call(
        functools.partial(mid_coupling_kernel, start, count),
        grid=(steps,),
        in_specs=[SMEM] + [ANY] * 4 + [pl.BlockSpec((depth, cols // steps), lambda s: (0, s))],
        out_specs=[tile, tile],
        out_shape=[
            jax.ShapeDtypeStruct((2 * width, cols), F32),
            jax.ShapeDtypeStruct((2 * width, cols), BF16),
        ],
        scratch_shapes=[pltpu.VMEM((2 * width, depth), BF16), pltpu.SemaphoreType.DMA((2, count))],
        compiler_params=params(),
        cost_estimate=cost(cols, depth, 2 * width),
    )(table, *sources, coup)


def leaf_first_kernel(chain, start, count, total, table_ref, order_ref, *refs):
    sources, (matrix_ref, *_, out_ref, bound_ref, sems) = refs[:total], refs[total:]

    @pl.when(pl.program_id(0) == 0)
    def _():
        targets = [bound_ref.at[:, pl.ds(i * BLOCK, BLOCK)] for i in range(count)]
        for i in range(count):
            start_fetch(sources, table_ref[chain, start + i], targets[i], sems.at[i])
        for i in range(count):
            pltpu.make_async_copy(sources[0].at[0], targets[i], sems.at[i]).wait()

    out_ref[0] = lax.dot_general(bound_ref[...], matrix_ref[...], NN, preferred_element_type=F32).astype(BF16)


def leaf_first(table, chain, start, count, sources, order, matrix, cols, after):
    width = sources[0].shape[1]
    depth = matrix.shape[0]
    return pl.pallas_call(
        functools.partial(leaf_first_kernel, chain, start, count, len(sources)),
        grid_spec=pltpu.PrefetchScalarGridSpec(
            num_scalar_prefetch=2,
            grid=(2,),
            in_specs=[ANY] * len(sources)
            + [pl.BlockSpec((depth, cols), lambda s, table, order: (0, order[s]))]
            + [ANY] * len(after),
            out_specs=[
                pl.BlockSpec((1, width, cols), lambda s, table, order: (s, 0, 0)),
                pl.BlockSpec((width, depth), lambda s, table, order: (0, 0)),
            ],
            scratch_shapes=[pltpu.SemaphoreType.DMA((count,))],
        ),
        out_shape=[
            jax.ShapeDtypeStruct((2, width, cols), BF16),
            jax.ShapeDtypeStruct((width, depth), BF16),
        ],
        compiler_params=params(),
        cost_estimate=cost(2 * cols, depth, width),
    )(table, order, *sources, matrix, *after)


def leaf_shift_kernel(chain, order_ref, keep_ref, got_ref, far_ref, rhs_ref, matrix_ref, *refs):
    out_ref, shift_ref = refs[-2:]

    @pl.when(pl.program_id(0) == 0)
    def _():
        width = shift_ref.shape[0]
        term = keep_ref[0] + got_ref[0].astype(F32) + far_ref[...].astype(F32)
        rhs = rhs_ref[0].T[chain * width : (chain + 1) * width]
        shift_ref[...] = (rhs.astype(F32) - term).astype(BF16)

    product = lax.dot_general(shift_ref[...], matrix_ref[...], NT, preferred_element_type=F32)
    out_ref[0] = product.astype(BF16)


def leaf_shift(chain, order, keep, got, far, rhs, matrix, after):
    _, width, depth = keep.shape
    one = pl.BlockSpec((1, width, depth), lambda s, order: (0, 0, 0))
    return pl.pallas_call(
        functools.partial(leaf_shift_kernel, chain),
        grid_spec=pltpu.PrefetchScalarGridSpec(
            num_scalar_prefetch=1,
            grid=(2,),
            in_specs=[
                one,
                one,
                pl.BlockSpec((width, depth), lambda s, order: (0, 0)),
                pl.BlockSpec(rhs.shape, lambda s, order: (0, 0, 0)),
                pl.BlockSpec((depth, depth), lambda s, order: (order[s], 0)),
            ]
            + [ANY] * len(after),
            out_specs=[
                pl.BlockSpec((1, width, depth), lambda s, order: (s, 0, 0)),
                pl.BlockSpec((width, depth), lambda s, order: (0, 0)),
            ],
        ),
        out_shape=[
            jax.ShapeDtypeStruct((2, width, depth), BF16),
            jax.ShapeDtypeStruct((width, depth), BF16),
        ],
        compiler_params=params(),
        cost_estimate=cost(2 * depth, depth, width),
    )(order, keep, got, far, rhs, matrix, *after)


def leaf_rest_kernel(dims, order_ref, value_ref, matrix_ref, out_ref):
    out_ref[0] = lax.dot_general(value_ref[...], matrix_ref[...], dims, preferred_element_type=F32)


def leaf_rest(order, dims, value, matrix, cols):
    width, depth = value.shape
    if dims is NN:
        spec = pl.BlockSpec((depth, cols), lambda s, order: (0, order[2 + s]))
    else:
        spec = pl.BlockSpec((cols, depth), lambda s, order: (order[2 + s], 0))
    return pl.pallas_call(
        functools.partial(leaf_rest_kernel, dims),
        grid_spec=pltpu.PrefetchScalarGridSpec(
            num_scalar_prefetch=1,
            grid=(2,),
            in_specs=[pl.BlockSpec((width, depth), lambda s, order: (0, 0)), spec],
            out_specs=pl.BlockSpec((1, width, cols), lambda s, order: (s, 0, 0)),
        ),
        out_shape=jax.ShapeDtypeStruct((2, width, cols), F32),
        compiler_params=params(),
        cost_estimate=cost(2 * cols, depth, width),
    )(order, value, matrix)


def leaf_finish_kernel(*refs):
    *terms, out_ref = refs
    sums = [
        terms[3 * n][0] + terms[3 * n + 1][0].astype(F32) + terms[3 * n + 2][...].astype(F32)
        for n in range(len(terms) // 3)
    ]
    out_ref[0] = jnp.concatenate([part.astype(BF16) for part in sums], axis=0).T


def leaf_finish(terms):
    _, width, rows = terms[0][0].shape
    one = pl.BlockSpec((1, width, rows), lambda s: (0, 0, 0))
    flat = [part for chain in terms for part in chain]
    return pl.pallas_call(
        leaf_finish_kernel,
        grid=(1,),
        in_specs=[one, one, pl.BlockSpec((width, rows), lambda s: (0, 0))] * len(terms),
        out_specs=pl.BlockSpec((1, rows, width * len(terms)), lambda s: (0, 0, 0)),
        out_shape=jax.ShapeDtypeStruct((1, rows, width * len(terms)), BF16),
        compiler_params=params(),
    )(*flat)


def swap(value, axis, mask):
    return lax.ppermute(value, axis, [(i, i ^ mask) for i in range(lax.axis_size(axis))])


def add(*terms):
    return functools.reduce(jnp.add, [t.astype(F32) for t in terms])


def reduce_columns(send, keep, bits, early, step):
    for i, bit in enumerate(bits):
        got = swap(send, "col", bit)
        if i == step:
            got, early = lax.optimization_barrier((got, early))
        if i < len(bits) - 1:
            half = got.shape[0] // 2
            send = add(keep[half:], got[half:]).astype(BF16)
            keep = add(keep[:half], got[:half])
    return add(keep, got).astype(BF16), early


def turn_columns(values, turn):
    return lax.switch(turn, [lambda *v, k=k: tuple(swap(part, "col", k) for part in v) for k in range(1, 8)], *values)


def gather_columns(value, bits):
    for bit in reversed(bits):
        value = jnp.concatenate([value, swap(value, "col", bit)], axis=0)
    return value


def natural(parts):
    blocks = jnp.concatenate(parts, axis=1)
    return jnp.swapaxes(blocks, 1, 2).reshape(-1, blocks.shape[1])


def shards(
    dinv_root,
    rhs_root,
    dinv_mid,
    coup_mid,
    rhs_mid,
    dinv_leaf,
    coup_leaf,
    rhs_leaf,
    bounds_mid,
    bounds_leaf,
    parents,
):
    row_id = lax.axis_index("row")
    col_id = lax.axis_index("col")
    x, h = row_id // 2, row_id % 2
    place = jnp.stack([row_id, col_id]).astype(jnp.int32)
    local = dinv_root.shape[0] // BLOCK
    slot = local // 8
    leaf_slots = bounds_leaf.shape[1] // 4
    at = plan_layout(local, slot, leaf_slots)
    chains = range(len(CHAINS))

    order = pl.pallas_call(
        functools.partial(order_kernel, local, slot),
        out_shape=jax.ShapeDtypeStruct((local,), jnp.int32),
        in_specs=[SMEM] * 2,
        out_specs=SMEM,
        scratch_shapes=[pltpu.SMEM((4 * local,), jnp.int32)],
    )(place, bounds_mid)
    plan = pl.pallas_call(
        functools.partial(plan_kernel, local, slot, leaf_slots),
        out_shape=jax.ShapeDtypeStruct((len(CHAINS), at["size"]), jnp.int32),
        in_specs=[SMEM] * 4,
        out_specs=SMEM,
        scratch_shapes=[pltpu.SMEM((4 * local,), jnp.int32)] * 2
        + [pltpu.SMEM((len(CHAINS), 4 * local), jnp.int32), pltpu.SMEM((2 * local,), jnp.int32)],
    )(place, bounds_mid, bounds_leaf, parents)

    half = local // 2
    leaf_order = jnp.stack([2 * x + 1 - h, 2 * (1 - x) + 1 - h, 2 * x + h, 2 * (1 - x) + h]).astype(jnp.int32)
    leaf_cols = coup_leaf.shape[2] // 4

    halves = root_product(order, rhs_root, dinv_root)
    boundary = []
    for n in chains:
        got, plan = reduce_columns(*halves[n], CHAINS[n], plan, 0)
        picked = gather(plan, n, at["select"], slot, (got, swap(got, "row", 1), swap(got, "row", 2)))
        own = gather_columns(picked, CHAINS[n])
        boundary.append((own, swap(own, "row", 1)))

    term, half_term = mid_coupling(plan, at["mid"], [part for pair in boundary for part in pair], coup_mid)
    asked = [
        swap(gather(plan, n, at["send_root"], leaf_slots + slot, boundary[n], (half_term,)), "row", 2)
        for n in chains
    ]
    first, shift = mid_first(x, term, swap(half_term, "row", 1), rhs_mid, dinv_mid)
    rest = mid_rest(shift, dinv_mid)
    products = (first, rest, swap(first, "row", 1), swap(rest, "row", 1))
    width = shift.shape[0] // 2
    root_values, mid_parts, mine, away = [], [], [], []
    child = parents[col_id] == x
    for n in chains:
        part = (n * width, width)
        send = gather(plan, n, at["mid_order"] + half, half, products, part=part)
        keep = gather(plan, n, at["mid_order"], half, products, part=part)
        got, asked[n] = reduce_columns(send, keep, CHAINS[n], asked[n], 2)
        root_values.append(gather(plan, n, at["out"], slot, (*boundary[n], asked[n])))
        mid_parts.append(got)
        other = swap(got, "row", 2)
        mine.append(jnp.where(child, got, other))
        away.append(jnp.where(child, other, got))
    back = turn_columns(away, plan[0, at["turn"]])
    sources = []
    for n in chains:
        own = jnp.concatenate([mine[n], back[n]], axis=0)
        sources.append((*boundary[n], asked[n], own, swap(own, "row", 1)))

    def spread(step):
        for n in chains:
            mid_parts[n] = jnp.concatenate([mid_parts[n], swap(mid_parts[n], "col", CHAINS[n][2 - step])], axis=0)

    def join(value):
        value, mid_parts[:] = lax.optimization_barrier((value, list(mid_parts)))
        return value

    coup, inverse = coup_leaf[0], dinv_leaf[0]
    after = ()
    sums = []
    for n in chains:
        spread(n)
        send, bound = leaf_first(plan, n, at["leaf"], leaf_slots, sources[n], leaf_order, coup, leaf_cols, after)
        send = join(send)
        got = swap(send, "row", 1)
        keep = leaf_rest(leaf_order, NN, bound, coup, leaf_cols)
        part = add(keep[1], got[1]).astype(BF16)
        sums.append((keep, got, swap(part, "row", 2)))
        after = (part,)
    ends = []
    for n in chains:
        if n == 0:
            spread(2)
        else:
            mid_parts[:] = [(own, swap(own, "row", 1)) for own in mid_parts]
        send, shift = leaf_shift(n, leaf_order, *sums[n], rhs_leaf, inverse, after)
        send = join(send)
        got = swap(send, "row", 1)
        keep = leaf_rest(leaf_order, NT, shift, inverse, leaf_cols)
        part = add(keep[1], got[1]).astype(BF16)
        ends.append((keep, got, swap(part, "row", 2)))
        after = (part,)
    mid_values = [gather(plan, n, at["mid_out"], slot, mid_parts[n]) for n in chains]
    return (natural(root_values), natural(mid_values), leaf_finish(ends))


def solution(mesh):
    sizes = dict(mesh.shape)
    in_specs = (
        P("row", "col"),
        P("col", None),
        P("row", "col"),
        P("row", "col"),
        P(None, "col", None),
        P("col", None, "row"),
        P("col", "row", None),
        P("col", "row", None),
        P(),
        P(),
        P(),
    )
    out_specs = (P(("row", "col"), None), P(("row", "col"), None), P("col", "row", None))

    def run(*args):
        fronts, listed = args[8].shape
        blocks = args[0].shape[0] // BLOCK
        whole = fronts == 2 and fronts * listed == blocks and args[2].shape[0] == args[0].shape[0]
        fits = sizes["row"] == 4 and sizes["col"] == 8 and whole
        body = shards if fits else general_shards
        return jax.shard_map(body, mesh=mesh, in_specs=in_specs, out_specs=out_specs, check_vma=False)(*args)

    return run
```

```python
import functools

import jax
import jax.numpy as jnp
from jax import lax
from jax.experimental import pallas as pl
from jax.experimental.pallas import tpu as pltpu
from jax.sharding import PartitionSpec as P

BLOCK = 128
F32 = jnp.float32
BF16 = jnp.bfloat16
NT = (((1,), (1,)), ((), ()))
NN = (((1,), (0,)), ((), ()))


def partner(value, axis, distance):
    mask = 2**distance
    pairs = [(source, source ^ mask) for source in range(lax.axis_size(axis))]
    return lax.ppermute(value, axis, pairs)


def pick_blocks(shard_rows, wanted):
    block_count = shard_rows.shape[0] // BLOCK
    flat_blocks = shard_rows.reshape(block_count, BLOCK * shard_rows.shape[1])
    present = jnp.arange(block_count, dtype=jnp.int32)
    select = (wanted[:, None] == present[None, :]).astype(shard_rows.dtype)
    return jnp.dot(select, flat_blocks, preferred_element_type=F32)


def transposed_product(coupling, boundary):
    return lax.dot_general(coupling, boundary, (((0,), (0,)), ((), ())), preferred_element_type=F32)


def general_shards(
    dinv_root,
    rhs_root,
    dinv_mid,
    coup_mid,
    rhs_mid,
    dinv_leaf,
    coup_leaf,
    rhs_leaf,
    bounds_mid,
    bounds_leaf,
    parents,
):
    row_total = lax.axis_size("row")
    row_id = lax.axis_index("row")
    col_id = lax.axis_index("col")
    rhs_width = rhs_root.shape[1]
    root_total = dinv_root.shape[0] * row_total // BLOCK
    front_mid = row_id // 2
    half_index = row_id % 2
    half_blocks = bounds_mid.shape[1] // 2
    mid_all = lax.dynamic_slice_in_dim(bounds_mid, front_mid, 1, 0)[0]
    mid_list = lax.dynamic_slice_in_dim(mid_all, half_index * half_blocks, half_blocks, 0)
    leaf_all = lax.dynamic_slice_in_dim(bounds_leaf, col_id, 1, 0)[0]
    leaf_slots = leaf_all.shape[0] // row_total
    leaf_list = lax.dynamic_slice_in_dim(leaf_all, row_id * leaf_slots, leaf_slots, 0)
    wanted = jnp.concatenate([mid_list, leaf_list])
    root_values = lax.psum_scatter(
        jnp.dot(dinv_root, rhs_root, preferred_element_type=F32),
        "col",
        scatter_dimension=0,
        tiled=True,
    ).astype(BF16)
    picked = pick_blocks(lax.all_gather(root_values, ("row", "col"), axis=0, tiled=True), wanted)
    bound_mid = picked[:half_blocks].reshape(half_blocks * BLOCK, rhs_width).astype(BF16)
    root_side = picked[half_blocks:]
    mid_part = transposed_product(coup_mid, bound_mid)
    mid_terms = mid_part + partner(mid_part, "row", 0)
    rhs_here = lax.dynamic_slice_in_dim(rhs_mid, front_mid, 1, 0)[0]
    shift_mid = (rhs_here - mid_terms).astype(BF16)
    mid_values = lax.psum_scatter(
        jnp.dot(dinv_mid, shift_mid, preferred_element_type=F32),
        "col",
        scatter_dimension=0,
        tiled=True,
    ).astype(BF16)
    half_rows = lax.all_gather(mid_values, "col", axis=0, tiled=True)
    half_count = half_rows.shape[0] // BLOCK
    half_flat = half_rows.reshape(half_count, BLOCK * rhs_width)
    local_ids = leaf_all - root_total - half_index * half_count
    owns_parent = lax.dynamic_slice_in_dim(parents, col_id, 1, 0)[0] == front_mid
    choose = (
        (local_ids[:, None] == jnp.arange(half_count, dtype=jnp.int32)[None, :]) & owns_parent
    ).astype(BF16)
    from_parent = lax.psum_scatter(
        jnp.dot(choose, half_flat, preferred_element_type=F32).astype(BF16),
        "row",
        scatter_dimension=0,
        tiled=True,
    ).astype(F32)
    bound_leaf = (root_side + from_parent).reshape(leaf_slots * BLOCK, rhs_width).astype(BF16)
    leaf_sum = lax.psum_scatter(
        transposed_product(coup_leaf[0], bound_leaf), "row", scatter_dimension=0, tiled=True
    )
    shift_leaf = (rhs_leaf[0] - leaf_sum).astype(BF16)
    leaf_values = lax.psum_scatter(
        jnp.dot(dinv_leaf[0], shift_leaf, preferred_element_type=F32),
        "row",
        scatter_dimension=0,
        tiled=True,
    ).astype(BF16)
    return (root_values, mid_values, leaf_values[None])


SMEM = pl.BlockSpec(memory_space=pltpu.SMEM)
VMEM = pl.BlockSpec(memory_space=pltpu.VMEM)
ANY = pl.BlockSpec(memory_space=pl.ANY)
MIB = 1024 * 1024
ORDERS = ((1, 2, 4), (2, 1, 4))
CHAINS = (0, 1)


def params(mib):
    return pltpu.CompilerParams(vmem_limit_bytes=mib * MIB)


def cost(rows, depth, width):
    return pl.CostEstimate(flops=2 * rows * depth * width, bytes_accessed=2 * rows * depth, transcendentals=0)


def loop(count, body):
    def step(i, carry):
        body(i)
        return carry

    lax.fori_loop(0, count, step, 0)


def place_of(chip, col, bits, slot):
    far = chip ^ col
    high, mid, low = (((far & bit) != 0).astype(jnp.int32) for bit in bits)
    return (4 * high + 2 * mid + low) * slot


def chips_in_order(col, bits):
    return [col ^ sum(bit for bit, shift in zip(bits, (4, 2, 1)) if t & shift) for t in range(8)]


def mark_fronts(bounds_ref, front):
    def body(j):
        front[bounds_ref[0, j]] = 0
        front[bounds_ref[1, j]] = 1

    loop(bounds_ref.shape[1], body)


def order_kernel(local, slot, place_ref, bounds_ref, out_ref, front):
    row, col = place_ref[0], place_ref[1]
    first = row * local
    mark_fronts(bounds_ref, front)
    before = lax.fori_loop(0, first, lambda v, s: s + 1 - front[v], jnp.int32(0))
    zeros = lax.fori_loop(0, local, lambda i, s: s + 1 - front[first + i], jnp.int32(0))

    def body(i, carry):
        low, high = carry
        kind = front[first + i]
        rank = jnp.where(kind == 0, low, zeros + high)
        out_ref[place_of((before + rank) & 7, col, ORDERS[0], slot) + (rank >> 3)] = i
        return low + 1 - kind, high + kind

    lax.fori_loop(0, local, body, (jnp.int32(0), jnp.int32(0)))


def plan_layout(local, slot, leaf_slots):
    at = {}
    size = 0
    for name, count in (
        ("select", slot),
        ("mid", local),
        ("send_root", leaf_slots + slot),
        ("leaf", leaf_slots),
        ("out", slot),
        ("mid_order", local),
        ("mid_out", slot),
        ("mid_send", slot),
        ("turn", 1),
    ):
        at[name] = size
        size += count
    at["size"] = size
    return at


def plan_kernel(local, slot, leaf_slots, place_ref, bounds_ref, leaf_ref, parents_ref, out_ref, front, ident, where, record):
    row, col = place_ref[0], place_ref[1]
    x, h = row // 2, row % 2
    total = 4 * local
    mark_fronts(bounds_ref, front)
    chains = range(len(ORDERS))
    at = plan_layout(local, slot, leaf_slots)

    def per_row(r, before):
        zeros = lax.fori_loop(0, local, lambda i, s: s + 1 - front[r * local + i], jnp.int32(0))

        def body(i, carry):
            low, high = carry
            kind = front[r * local + i]
            rank = jnp.where(kind == 0, low, zeros + high)
            chip = (before + rank) & 7
            ident[r * local + chip * slot + (rank >> 3)] = r * local + i
            return low + 1 - kind, high + kind

        lax.fori_loop(0, local, body, (jnp.int32(0), jnp.int32(0)))
        return before + zeros

    lax.fori_loop(0, 4, per_row, jnp.int32(0))

    def clear(v):
        for n in chains:
            where[n, v] = 0

    loop(total, clear)

    def per_chip(chip, _):
        here = chip == col
        near = [place_of(chip, col, bits, slot) for bits in ORDERS]

        def put(core, count, block, code):
            for n in chains:
                where[n, block] = (core ^ h) * local + near[n] + count

            @pl.when(here & (core == h))
            def _():
                for n in chains:
                    out_ref[n, count] = code

        def from_far(step, carry):
            count0, count1 = carry
            core, k = step // slot, step % slot
            block = ident[(2 * (1 - x) + core) * local + chip * slot + k]
            taken = front[block] == x
            count = jnp.where(core == 0, count0, count1)

            @pl.when(taken)
            def _():
                put(core, count, block, 2 * slot + k)

            add = taken.astype(jnp.int32)
            return count0 + jnp.where(core == 0, add, 0), count1 + jnp.where(core == 0, 0, add)

        counts = lax.fori_loop(0, 2 * slot, from_far, (jnp.int32(0), jnp.int32(0)))

        def from_near(step, carry):
            count0, count1 = carry
            owner, k = step // slot, step % slot
            block = ident[(2 * x + owner) * local + chip * slot + k]
            taken = front[block] == x
            core = (count0 >= slot).astype(jnp.int32)
            count = jnp.where(core == 0, count0, count1)

            @pl.when(taken)
            def _():
                put(core, count, block, (owner ^ core) * slot + k)

            add = taken.astype(jnp.int32)
            return count0 + jnp.where(core == 0, add, 0), count1 + jnp.where(core == 0, 0, add)

        lax.fori_loop(0, 2 * slot, from_near, counts)
        return 0

    lax.fori_loop(0, 8, per_chip, 0)

    def mid_list(j):
        block = bounds_ref[x, h * local + j]
        for n in chains:
            out_ref[n, at["mid"] + j] = where[n, block]

    loop(local, mid_list)
    far = 2 * (1 - x) + h
    turn = jnp.int32(6)
    for k in range(7, 0, -1):
        apart = [(parents_ref[c] != parents_ref[c ^ k]).astype(jnp.int32) for c in range(8)]
        turn = jnp.where(functools.reduce(jnp.multiply, apart) == 1, k - 1, turn)
    out_ref[0, at["turn"]] = turn
    listed = 4 * leaf_slots

    def per_leaf(leaf, _):
        @pl.when(parents_ref[leaf] == x)
        def _():
            def body(j, rank):
                block = leaf_ref[leaf, j]
                taken = block >= total

                @pl.when(taken)
                def _():
                    record[block - total] = leaf * 4 * slot + rank

                return rank + taken.astype(jnp.int32)

            lax.fori_loop(0, listed, body, jnp.int32(0))

        return 0

    lax.fori_loop(0, 8, per_leaf, 0)

    def spot(block):
        leaf, rank = record[block] // (4 * slot), record[block] % (4 * slot)
        chip = jnp.where(rank < 2 * slot, leaf, leaf ^ (turn + 1))
        return chip, rank // slot % 2, rank % slot

    def mid_orders(block):
        chip, core, k = spot(block)

        @pl.when(core == h)
        def _():
            for n in chains:
                place = place_of(chip, col, ORDERS[n], slot) + k
                out_ref[n, at["mid_order"] + place] = (block // local ^ h) * local + block % local

    loop(2 * local, mid_orders)

    def mid_outs(j):
        chip, core, k = spot(h * local + col * slot + j)
        out_ref[0, at["mid_out"] + j] = jnp.where(core == h, chip * slot + k, local + j)
        chip, core, k = spot((1 - h) * local + col * slot + j)
        out_ref[0, at["mid_send"] + j] = chip * slot + k

    loop(slot, mid_outs)

    def sends(j):
        asked = leaf_ref[col, far * leaf_slots + j]
        for n in chains:
            out_ref[n, at["send_root"] + j] = where[n, jnp.minimum(asked, total - 1)]

    loop(leaf_slots, sends)

    def count(j, rank):
        return rank + (leaf_ref[col, j] >= total).astype(jnp.int32)

    def lists(j, rank):
        held = leaf_ref[col, row * leaf_slots + j]
        low = jnp.minimum(held, total - 1)
        place = (rank // slot % 2 ^ h) * 2 * slot + rank // (2 * slot) * slot + rank % slot
        for n in chains:
            from_root = jnp.where(front[low] == x, where[n, low], 2 * local + j)
            from_mid = 2 * local + leaf_slots + slot + place
            out_ref[n, at["leaf"] + j] = jnp.where(held < total, from_root, from_mid)
        return count(row * leaf_slots + j, rank)

    lax.fori_loop(0, leaf_slots, lists, lax.fori_loop(0, row * leaf_slots, count, jnp.int32(0)))

    def outs(j):
        asked = far * local + col * slot + j
        held = row * local + col * slot + j
        for n in chains:
            out_ref[n, at["send_root"] + leaf_slots + j] = where[n, asked]
            out_ref[n, at["out"] + j] = jnp.where(front[held] == x, where[n, held], 2 * local + leaf_slots + j)

    loop(slot, outs)


def start_fetch(sources, code, target, sem):
    base = 0
    for source, rows in sources:
        count = source.shape[0]

        @pl.when((code >= base) & (code < base + count))
        def _(source=source, base=base, rows=rows):
            pltpu.make_async_copy(source.at[code - base, rows], target, sem).start()

        base += count


def flatten(parts):
    arrays, plans = [], []
    for order, width, sources in parts:
        plan = []
        for array, first in sources:
            number = next((i for i, known in enumerate(arrays) if known is array), len(arrays))
            if number == len(arrays):
                arrays.append(array)
            plan.append((number, first))
        plans.append((order, width, tuple(plan)))
    return arrays, tuple(plans)


def fetch_all(plans, start, count, table_ref, refs, target, sems):
    def each(act):
        first = 0
        for p, (order, width, plan) in enumerate(plans):
            for i in range(count):
                place = target(i, p, first, width)
                act(p, i, order, [(refs[k], pl.ds(row, width)) for k, row in plan], place)
            first += width

    def begin(p, i, order, sources, place):
        start_fetch(sources, table_ref[order, start + i], place, sems.at[p, i])

    def end(p, i, order, sources, place):
        blocks, rows = sources[0]
        pltpu.make_async_copy(blocks.at[0, rows], place, sems.at[p, i]).wait()

    each(begin)
    each(end)


def gather_kernel(plans, start, count, total, split, table_ref, *refs):
    outs, sems = refs[-1 - (len(plans) if split else 1) : -1], refs[-1]

    def target(i, p, first, width):
        return outs[p].at[i] if split else outs[0].at[i, pl.ds(first, width)]

    fetch_all(plans, start, count, table_ref, refs[:total], target, sems)


def gather(table, start, count, parts, after=(), split=False):
    arrays, plans = flatten(parts)
    widths = [part[1] for part in plans] if split else [sum(part[1] for part in plans)]
    outs = pl.pallas_call(
        functools.partial(gather_kernel, plans, start, count, len(arrays), split),
        out_shape=[jax.ShapeDtypeStruct((count, width, BLOCK), BF16) for width in widths],
        in_specs=[SMEM] + [ANY] * (len(arrays) + len(after)),
        out_specs=[VMEM] * len(widths),
        scratch_shapes=[pltpu.SemaphoreType.DMA((len(plans), count))],
        compiler_params=params(10),
    )(table, *arrays, *after)
    return outs if split else outs[0]


def store_blocks(ref, result):
    for i in range(ref.shape[0]):
        ref[i] = result[:, i * BLOCK : (i + 1) * BLOCK].astype(ref.dtype)


def root_product_kernel(parts, last, order_ref, value_ref, *refs):
    blocks, outs, turned = refs[:parts], refs[parts:-1], refs[-1]
    step = pl.program_id(0)

    @pl.when(step == 0)
    def _():
        turned[...] = value_ref[...].T

    matrix = jnp.concatenate([b[...] for b in blocks], axis=0)
    result = lax.dot_general(turned[...], matrix, NT, preferred_element_type=F32)
    width = result.shape[0] // len(CHAINS)
    for n, order in enumerate(CHAINS):
        part = result[n * width : (n + 1) * width]
        if last:
            store_blocks(outs[n], part)
            continue
        next_step = 2 - order

        @pl.when(step != next_step)
        def _(n=n, part=part):
            store_blocks(outs[2 * n], part)

        @pl.when(step == next_step)
        def _(n=n, part=part):
            store_blocks(outs[2 * n + 1], part)


def root_product(order, value, matrix, last):
    depth, width = value.shape
    local = matrix.shape[0] // BLOCK
    parts = local // 4
    base = 0 if last else 3

    def spec(i):
        return pl.BlockSpec((BLOCK, depth), lambda s, order: (order[parts * (base - s) + i], 0))

    part = width // len(CHAINS)
    block = (parts, part, BLOCK)
    fixed = pl.BlockSpec(block, lambda s, order: (0, 0, 0))
    rest = jax.ShapeDtypeStruct(block, F32)
    if last:
        out_specs, out_shape = [fixed] * len(CHAINS), [rest] * len(CHAINS)
    else:
        first = pl.BlockSpec(block, lambda s, order: (jnp.where(s == 0, 1, 0), 0, 0))
        out_specs = [first, fixed] * len(CHAINS)
        out_shape = [jax.ShapeDtypeStruct((local // 2, part, BLOCK), BF16), rest] * len(CHAINS)
    return pl.pallas_call(
        functools.partial(root_product_kernel, parts, last),
        grid_spec=pltpu.PrefetchScalarGridSpec(
            num_scalar_prefetch=1,
            grid=(1 if last else 3,),
            in_specs=[pl.BlockSpec((depth, width), lambda s, order: (0, 0))] + [spec(i) for i in range(parts)],
            out_specs=out_specs,
            scratch_shapes=[pltpu.VMEM((width, depth), BF16)],
        ),
        out_shape=out_shape,
        compiler_params=params(60),
        cost_estimate=cost(matrix.shape[0] // 4 * (1 if last else 3), depth, width),
    )(order, value, *([matrix] * parts))


def mid_first_kernel(front_ref, term_ref, got_ref, rhs_ref, matrix_ref, *refs):
    out_ref, shift_ref = refs[-2:]

    @pl.when(pl.program_id(0) == 0)
    def _():
        shift_ref[...] = (rhs_ref[0].T.astype(F32) - (term_ref[...] + got_ref[...].astype(F32))).astype(BF16)

    store_blocks(out_ref, lax.dot_general(shift_ref[...], matrix_ref[...], NT, preferred_element_type=F32))


def mid_rest_kernel(shift_ref, matrix_ref, out_ref):
    store_blocks(out_ref, lax.dot_general(shift_ref[...], matrix_ref[...], NT, preferred_element_type=F32))


def mid_first(front, term, got, rhs, matrix, after):
    width, depth = term.shape
    half = matrix.shape[0] // BLOCK // 2
    whole = pl.BlockSpec((width, depth), lambda s, front: (0, 0))
    return pl.pallas_call(
        mid_first_kernel,
        grid_spec=pltpu.PrefetchScalarGridSpec(
            num_scalar_prefetch=1,
            grid=(2,),
            in_specs=[
                whole,
                whole,
                pl.BlockSpec((1, depth, width), lambda s, front: (front[0], 0, 0)),
                pl.BlockSpec((half // 2 * BLOCK, depth), lambda s, front: (s, 0)),
            ]
            + [ANY] * len(after),
            out_specs=[pl.BlockSpec((half // 2, width, BLOCK), lambda s, front: (s, 0, 0)), whole],
        ),
        out_shape=[
            jax.ShapeDtypeStruct((half, width, BLOCK), BF16),
            jax.ShapeDtypeStruct((width, depth), BF16),
        ],
        compiler_params=params(60),
        cost_estimate=cost(half * BLOCK, depth, width),
    )(front.reshape(1), term, got, rhs, matrix, *after)


def mid_rest(shift, matrix):
    width, depth = shift.shape
    half = matrix.shape[0] // BLOCK // 2
    return pl.pallas_call(
        mid_rest_kernel,
        grid=(2,),
        in_specs=[
            pl.BlockSpec((width, depth), lambda s: (0, 0)),
            pl.BlockSpec((half // 2 * BLOCK, depth), lambda s: (2 + s, 0)),
        ],
        out_specs=pl.BlockSpec((half // 2, width, BLOCK), lambda s: (s, 0, 0)),
        out_shape=jax.ShapeDtypeStruct((half, width, BLOCK), BF16),
        compiler_params=params(60),
        cost_estimate=cost(half * BLOCK, depth, width),
    )(shift, matrix)


def mid_coupling_kernel(plans, start, count, total, table_ref, *refs):
    coup_ref, out_ref, send_ref, bound, sems = refs[total:]

    def target(i, p, first, width):
        return bound.at[pl.ds(first, width), pl.ds(i * BLOCK, BLOCK)]

    @pl.when(pl.program_id(0) == 0)
    def _():
        fetch_all(plans, start, count, table_ref, refs[:total], target, sems)

    product = lax.dot_general(bound[...], coup_ref[...], NN, preferred_element_type=F32)
    out_ref[...] = product
    send_ref[...] = product.astype(BF16)


def mid_coupling(table, start, parts, coup, steps=4):
    arrays, plans = flatten(parts)
    width = sum(part[1] for part in plans)
    depth, cols = coup.shape
    count = depth // BLOCK
    tile = pl.BlockSpec((width, cols // steps), lambda s: (0, s))
    return pl.pallas_call(
        functools.partial(mid_coupling_kernel, plans, start, count, len(arrays)),
        grid=(steps,),
        in_specs=[SMEM] + [ANY] * len(arrays) + [pl.BlockSpec((depth, cols // steps), lambda s: (0, s))],
        out_specs=[tile, tile],
        out_shape=[jax.ShapeDtypeStruct((width, cols), F32), jax.ShapeDtypeStruct((width, cols), BF16)],
        scratch_shapes=[pltpu.VMEM((width, depth), BF16), pltpu.SemaphoreType.DMA((len(plans), count))],
        compiler_params=params(24),
        cost_estimate=cost(cols, depth, width),
    )(table, *arrays, coup)


def leaf_first_kernel(plans, start, count, total, table_ref, order_ref, *refs):
    matrix_ref, out_ref, bound_ref, sems = refs[total:]

    def target(i, p, first, width):
        return bound_ref.at[pl.ds(first, width), pl.ds(i * BLOCK, BLOCK)]

    @pl.when(pl.program_id(0) == 0)
    def _():
        fetch_all(plans, start, count, table_ref, refs[:total], target, sems)

    out_ref[0] = lax.dot_general(bound_ref[...], matrix_ref[...], NN, preferred_element_type=F32).astype(BF16)


def leaf_first(table, start, parts, order, matrix, cols):
    arrays, plans = flatten(parts)
    width = sum(part[1] for part in plans)
    depth = matrix.shape[0]
    count = depth // BLOCK
    return pl.pallas_call(
        functools.partial(leaf_first_kernel, plans, start, count, len(arrays)),
        grid_spec=pltpu.PrefetchScalarGridSpec(
            num_scalar_prefetch=2,
            grid=(2,),
            in_specs=[ANY] * len(arrays) + [pl.BlockSpec((depth, cols), lambda s, table, order: (0, order[s]))],
            out_specs=[
                pl.BlockSpec((1, width, cols), lambda s, table, order: (s, 0, 0)),
                pl.BlockSpec((width, depth), lambda s, table, order: (0, 0)),
            ],
            scratch_shapes=[pltpu.SemaphoreType.DMA((len(plans), count))],
        ),
        out_shape=[
            jax.ShapeDtypeStruct((2, width, cols), BF16),
            jax.ShapeDtypeStruct((width, depth), BF16),
        ],
        compiler_params=params(60),
        cost_estimate=cost(2 * cols, depth, width),
    )(table, order, *arrays, matrix)


def leaf_shift_kernel(order_ref, keep_ref, got_ref, far_ref, rhs_ref, matrix_ref, *refs):
    out_ref, shift_ref = refs[-2:]

    @pl.when(pl.program_id(0) == 0)
    def _():
        term = keep_ref[0] + got_ref[0].astype(F32) + far_ref[...].astype(F32)
        shift_ref[...] = (rhs_ref[0].T.astype(F32) - term).astype(BF16)

    product = lax.dot_general(shift_ref[...], matrix_ref[...], NT, preferred_element_type=F32)
    out_ref[0] = product.astype(BF16)


def leaf_shift(order, keep, got, far, rhs, matrix, after):
    _, width, depth = keep.shape
    one = pl.BlockSpec((1, width, depth), lambda s, order: (0, 0, 0))
    flat = pl.BlockSpec((width, depth), lambda s, order: (0, 0))
    return pl.pallas_call(
        leaf_shift_kernel,
        grid_spec=pltpu.PrefetchScalarGridSpec(
            num_scalar_prefetch=1,
            grid=(2,),
            in_specs=[
                one,
                one,
                flat,
                pl.BlockSpec(rhs.shape, lambda s, order: (0, 0, 0)),
                pl.BlockSpec((depth, depth), lambda s, order: (order[s], 0)),
            ]
            + [ANY] * len(after),
            out_specs=[pl.BlockSpec((1, width, depth), lambda s, order: (s, 0, 0)), flat],
        ),
        out_shape=[
            jax.ShapeDtypeStruct((2, width, depth), BF16),
            jax.ShapeDtypeStruct((width, depth), BF16),
        ],
        compiler_params=params(60),
        cost_estimate=cost(2 * depth, depth, width),
    )(order, keep, got, far, rhs, matrix, *after)


def leaf_rest_kernel(dims, order_ref, value_ref, matrix_ref, out_ref):
    out_ref[0] = lax.dot_general(value_ref[...], matrix_ref[...], dims, preferred_element_type=F32)


def leaf_rest(order, dims, value, matrix, cols, mib):
    width, depth = value.shape
    if dims is NN:
        spec = pl.BlockSpec((depth, cols), lambda s, order: (0, order[2 + s]))
    else:
        spec = pl.BlockSpec((cols, depth), lambda s, order: (order[2 + s], 0))
    return pl.pallas_call(
        functools.partial(leaf_rest_kernel, dims),
        grid_spec=pltpu.PrefetchScalarGridSpec(
            num_scalar_prefetch=1,
            grid=(2,),
            in_specs=[pl.BlockSpec((width, depth), lambda s, order: (0, 0)), spec],
            out_specs=pl.BlockSpec((1, width, cols), lambda s, order: (s, 0, 0)),
        ),
        out_shape=jax.ShapeDtypeStruct((2, width, cols), F32),
        compiler_params=params(mib),
        cost_estimate=cost(2 * cols, depth, width),
    )(order, value, matrix)


def leaf_finish_kernel(keep_ref, got_ref, far_ref, *refs):
    total = keep_ref[0] + got_ref[0].astype(F32) + far_ref[...].astype(F32)
    refs[-1][0] = total.astype(BF16).T


def leaf_finish(keep, got, far, after):
    _, width, rows = keep.shape
    one = pl.BlockSpec((1, width, rows), lambda s: (0, 0, 0))
    return pl.pallas_call(
        leaf_finish_kernel,
        grid=(1,),
        in_specs=[one, one, pl.BlockSpec((width, rows), lambda s: (0, 0))] + [ANY] * len(after),
        out_specs=pl.BlockSpec((1, rows, width), lambda s: (0, 0, 0)),
        out_shape=jax.ShapeDtypeStruct((1, rows, width), BF16),
        compiler_params=params(60),
    )(keep, got, far, *after)


def swap(value, axis, mask):
    return lax.ppermute(value, axis, [(i, i ^ mask) for i in range(lax.axis_size(axis))])


def add(*terms):
    return functools.reduce(jnp.add, [t.astype(F32) for t in terms])


def tie(value, others):
    value, others[:] = lax.optimization_barrier((value, list(others)))
    return value


def reduce_columns(send, hold, keep, bits, early, step):
    for i, bit in enumerate(bits):
        got = swap(send, "col", bit)
        if i == step:
            got = tie(got, early)
        if i < len(bits) - 1:
            half = got.shape[0] // 2
            send = add(hold, got[half:]).astype(BF16)
            keep = add(keep, got[:half])
        if i < len(bits) - 2:
            hold, keep = keep[half // 2 :], keep[: half // 2]
    return add(keep, got).astype(BF16)


def turn_columns(value, turn):
    return lax.switch(turn, [lambda v, k=k: swap(v, "col", k) for k in range(1, 8)], value)


def gather_columns(value, bits):
    for bit in (bits[2], bits[1]):
        value = jnp.concatenate([value, swap(value, "col", bit)], axis=0)
    far = swap(value, "col", bits[0])
    return [value, far, swap(value, "row", 1), swap(far, "row", 1)]


def natural(blocks):
    return jnp.swapaxes(blocks, 1, 2).reshape(-1, blocks.shape[1])


def shards(
    dinv_root,
    rhs_root,
    dinv_mid,
    coup_mid,
    rhs_mid,
    dinv_leaf,
    coup_leaf,
    rhs_leaf,
    bounds_mid,
    bounds_leaf,
    parents,
):
    row_id = lax.axis_index("row")
    col_id = lax.axis_index("col")
    x, h = row_id // 2, row_id % 2
    place = jnp.stack([row_id, col_id]).astype(jnp.int32)
    local = dinv_root.shape[0] // BLOCK
    slot = local // 8
    leaf_slots = bounds_leaf.shape[1] // 4
    at = plan_layout(local, slot, leaf_slots)

    order = pl.pallas_call(
        functools.partial(order_kernel, local, slot),
        out_shape=jax.ShapeDtypeStruct((local,), jnp.int32),
        in_specs=[SMEM] * 2,
        out_specs=SMEM,
        scratch_shapes=[pltpu.SMEM((4 * local,), jnp.int32)],
    )(place, bounds_mid)
    plan = pl.pallas_call(
        functools.partial(plan_kernel, local, slot, leaf_slots),
        out_shape=jax.ShapeDtypeStruct((len(ORDERS), at["size"]), jnp.int32),
        in_specs=[SMEM] * 4,
        out_specs=SMEM,
        scratch_shapes=[pltpu.SMEM((4 * local,), jnp.int32)] * 2
        + [pltpu.SMEM((len(ORDERS), 4 * local), jnp.int32), pltpu.SMEM((2 * local,), jnp.int32)],
    )(place, bounds_mid, bounds_leaf, parents)

    half, quarter = local // 2, local // 4
    leaf_order = jnp.stack([2 * x + 1 - h, 2 * (1 - x) + 1 - h, 2 * x + h, 2 * (1 - x) + h]).astype(jnp.int32)
    leaf_cols = coup_leaf.shape[2] // 4
    width = rhs_root.shape[1] // len(CHAINS)
    chains = range(len(CHAINS))

    def whole(arrays):
        return [(array, 0) for array in arrays]

    def rows(arrays, n):
        return [(array, n * width) for array in arrays]

    first = root_product(order, rhs_root, dinv_root, False)
    last = root_product(order, rhs_root, dinv_root, True)
    tables = [plan]
    boundary = []
    for n, kind in enumerate(CHAINS):
        got = reduce_columns(*first[2 * n : 2 * n + 2], last[n], ORDERS[kind], tables, 0)
        picked = [(kind, width, whole((got, swap(got, "row", 1), swap(got, "row", 2))))]
        boundary.append(gather_columns(gather(tables[0], at["select"], slot, picked), ORDERS[kind]))
    plan = tables[0]
    parts = [(kind, width, whole(boundary[n])) for n, kind in enumerate(CHAINS)]

    term, half_term = mid_coupling(plan, at["mid"], parts, coup_mid)
    front, shift = mid_first(x, term, swap(half_term, "row", 1), rhs_mid, dinv_mid, ())
    back = mid_rest(shift, dinv_mid)
    asking = gather(plan, at["send_root"], leaf_slots + slot, parts, (back,), split=True)
    asked = [[swap(part, "row", 2)] for part in asking]
    products = (front, back, swap(front, "row", 1), swap(back, "row", 1))
    parts = [(kind, width, rows(products, n)) for n, kind in enumerate(CHAINS)]
    sends = gather(plan, at["mid_order"] + half, half, parts, split=True)
    keeps = gather(plan, at["mid_order"], half, parts, (sends[0],), split=True)
    got = []
    for n, kind in enumerate(CHAINS):
        hold, keep = keeps[n][quarter:], keeps[n][:quarter]
        early = [] if n == 0 else asked[0]
        got.append(reduce_columns(sends[n], hold, keep, ORDERS[kind], early, 1))
    got = tie(jnp.concatenate(got, axis=1), asked[1])
    other = swap(got, "row", 2)
    child = parents[col_id] == x
    mine, away = jnp.where(child, got, other), jnp.where(child, other, got)
    own = jnp.concatenate([mine, turn_columns(away, plan[0, at["turn"]])], axis=0)
    sib = swap(own, "row", 1)
    sources = [(kind, width, whole((*boundary[n], *asked[n])) + rows((own, sib), n)) for n, kind in enumerate(CHAINS)]
    mid = lax.all_gather(got, "col", axis=0, tiled=True)

    def reduce_rows(send, keep):
        got = swap(send, "row", 1)
        far = swap(add(keep[1], got[1]).astype(BF16), "row", 2)
        return keep, got, far

    send, bound = leaf_first(plan, at["leaf"], sources, leaf_order, coup_leaf[0], leaf_cols)
    terms = reduce_rows(send, leaf_rest(leaf_order, NN, bound, coup_leaf[0], leaf_cols, 60))
    held = [(kind, width, whole((*boundary[n], *asked[n]))) for n, kind in enumerate(CHAINS)]
    root_values = gather(plan, at["out"], slot, held)
    root_values = natural(root_values)
    send, shift = leaf_shift(leaf_order, *terms, rhs_leaf, dinv_leaf[0], (root_values,))
    terms = reduce_rows(send, leaf_rest(leaf_order, NT, shift, dinv_leaf[0], leaf_cols, 60))
    joint = len(CHAINS) * width
    wanted = gather(plan, at["mid_send"], slot, [(0, joint, whole((mid,)))])
    mid_values = gather(plan, at["mid_out"], slot, [(0, joint, whole((mid, swap(wanted, "row", 1))))])
    mid_values = natural(mid_values)
    return (root_values, mid_values, leaf_finish(*terms, (mid_values,)))


def solution(mesh):
    sizes = dict(mesh.shape)
    in_specs = (
        P("row", "col"),
        P("col", None),
        P("row", "col"),
        P("row", "col"),
        P(None, "col", None),
        P("col", None, "row"),
        P("col", "row", None),
        P("col", "row", None),
        P(),
        P(),
        P(),
    )
    out_specs = (P(("row", "col"), None), P(("row", "col"), None), P("col", "row", None))

    def run(*args):
        fronts, listed = args[8].shape
        blocks = args[0].shape[0] // BLOCK
        whole = fronts == 2 and fronts * listed == blocks and args[2].shape[0] == args[0].shape[0]
        fits = sizes["row"] == 4 and sizes["col"] == 8 and whole
        body = shards if fits else general_shards
        return jax.shard_map(body, mesh=mesh, in_specs=in_specs, out_specs=out_specs, check_vma=False)(*args)

    return run
```

```python
import functools

import jax
import jax.numpy as jnp
from jax import lax
from jax.experimental import pallas as pl
from jax.experimental.pallas import tpu as pltpu
from jax.sharding import PartitionSpec as P

BLOCK = 128
F32 = jnp.float32
BF16 = jnp.bfloat16
NT = (((1,), (1,)), ((), ()))
NN = (((1,), (0,)), ((), ()))


def partner(value, axis, distance):
    mask = 2**distance
    pairs = [(source, source ^ mask) for source in range(lax.axis_size(axis))]
    return lax.ppermute(value, axis, pairs)


def pick_blocks(shard_rows, wanted):
    block_count = shard_rows.shape[0] // BLOCK
    flat_blocks = shard_rows.reshape(block_count, BLOCK * shard_rows.shape[1])
    present = jnp.arange(block_count, dtype=jnp.int32)
    select = (wanted[:, None] == present[None, :]).astype(shard_rows.dtype)
    return jnp.dot(select, flat_blocks, preferred_element_type=F32)


def transposed_product(coupling, boundary):
    return lax.dot_general(coupling, boundary, (((0,), (0,)), ((), ())), preferred_element_type=F32)


def general_shards(
    dinv_root,
    rhs_root,
    dinv_mid,
    coup_mid,
    rhs_mid,
    dinv_leaf,
    coup_leaf,
    rhs_leaf,
    bounds_mid,
    bounds_leaf,
    parents,
):
    row_total = lax.axis_size("row")
    row_id = lax.axis_index("row")
    col_id = lax.axis_index("col")
    rhs_width = rhs_root.shape[1]
    root_total = dinv_root.shape[0] * row_total // BLOCK
    front_mid = row_id // 2
    half_index = row_id % 2
    half_blocks = bounds_mid.shape[1] // 2
    mid_all = lax.dynamic_slice_in_dim(bounds_mid, front_mid, 1, 0)[0]
    mid_list = lax.dynamic_slice_in_dim(mid_all, half_index * half_blocks, half_blocks, 0)
    leaf_all = lax.dynamic_slice_in_dim(bounds_leaf, col_id, 1, 0)[0]
    leaf_slots = leaf_all.shape[0] // row_total
    leaf_list = lax.dynamic_slice_in_dim(leaf_all, row_id * leaf_slots, leaf_slots, 0)
    wanted = jnp.concatenate([mid_list, leaf_list])
    root_values = lax.psum_scatter(
        jnp.dot(dinv_root, rhs_root, preferred_element_type=F32),
        "col",
        scatter_dimension=0,
        tiled=True,
    ).astype(BF16)
    picked = pick_blocks(lax.all_gather(root_values, ("row", "col"), axis=0, tiled=True), wanted)
    bound_mid = picked[:half_blocks].reshape(half_blocks * BLOCK, rhs_width).astype(BF16)
    root_side = picked[half_blocks:]
    mid_part = transposed_product(coup_mid, bound_mid)
    mid_terms = mid_part + partner(mid_part, "row", 0)
    rhs_here = lax.dynamic_slice_in_dim(rhs_mid, front_mid, 1, 0)[0]
    shift_mid = (rhs_here - mid_terms).astype(BF16)
    mid_values = lax.psum_scatter(
        jnp.dot(dinv_mid, shift_mid, preferred_element_type=F32),
        "col",
        scatter_dimension=0,
        tiled=True,
    ).astype(BF16)
    half_rows = lax.all_gather(mid_values, "col", axis=0, tiled=True)
    half_count = half_rows.shape[0] // BLOCK
    half_flat = half_rows.reshape(half_count, BLOCK * rhs_width)
    local_ids = leaf_all - root_total - half_index * half_count
    owns_parent = lax.dynamic_slice_in_dim(parents, col_id, 1, 0)[0] == front_mid
    choose = (
        (local_ids[:, None] == jnp.arange(half_count, dtype=jnp.int32)[None, :]) & owns_parent
    ).astype(BF16)
    from_parent = lax.psum_scatter(
        jnp.dot(choose, half_flat, preferred_element_type=F32).astype(BF16),
        "row",
        scatter_dimension=0,
        tiled=True,
    ).astype(F32)
    bound_leaf = (root_side + from_parent).reshape(leaf_slots * BLOCK, rhs_width).astype(BF16)
    leaf_sum = lax.psum_scatter(
        transposed_product(coup_leaf[0], bound_leaf), "row", scatter_dimension=0, tiled=True
    )
    shift_leaf = (rhs_leaf[0] - leaf_sum).astype(BF16)
    leaf_values = lax.psum_scatter(
        jnp.dot(dinv_leaf[0], shift_leaf, preferred_element_type=F32),
        "row",
        scatter_dimension=0,
        tiled=True,
    ).astype(BF16)
    return (root_values, mid_values, leaf_values[None])


SMEM = pl.BlockSpec(memory_space=pltpu.SMEM)
VMEM = pl.BlockSpec(memory_space=pltpu.VMEM)
ANY = pl.BlockSpec(memory_space=pl.ANY)
MIB = 1024 * 1024
ORDERS = ((1, 2, 4), (2, 1, 4))
CHAINS = (0, 1)


def params(mib):
    return pltpu.CompilerParams(vmem_limit_bytes=mib * MIB)


def cost(rows, depth, width):
    return pl.CostEstimate(flops=2 * rows * depth * width, bytes_accessed=2 * rows * depth, transcendentals=0)


def loop(count, body):
    def step(i, carry):
        body(i)
        return carry

    lax.fori_loop(0, count, step, 0)


def place_of(chip, col, bits, slot):
    far = chip ^ col
    high, mid, low = (((far & bit) != 0).astype(jnp.int32) for bit in bits)
    return (4 * high + 2 * mid + low) * slot


def chips_in_order(col, bits):
    return [col ^ sum(bit for bit, shift in zip(bits, (4, 2, 1)) if t & shift) for t in range(8)]


def mark_fronts(bounds_ref, front):
    def body(j):
        front[bounds_ref[0, j]] = 0
        front[bounds_ref[1, j]] = 1

    loop(bounds_ref.shape[1], body)


def order_kernel(local, slot, place_ref, bounds_ref, out_ref, front):
    row, col = place_ref[0], place_ref[1]
    first = row * local
    mark_fronts(bounds_ref, front)
    before = lax.fori_loop(0, first, lambda v, s: s + 1 - front[v], jnp.int32(0))
    zeros = lax.fori_loop(0, local, lambda i, s: s + 1 - front[first + i], jnp.int32(0))

    def body(i, carry):
        low, high = carry
        kind = front[first + i]
        rank = jnp.where(kind == 0, low, zeros + high)
        out_ref[place_of((before + rank) & 7, col, ORDERS[0], slot) + (rank >> 3)] = i
        return low + 1 - kind, high + kind

    lax.fori_loop(0, local, body, (jnp.int32(0), jnp.int32(0)))


def plan_layout(local, slot, leaf_slots):
    at = {}
    size = 0
    for name, count in (
        ("select", slot),
        ("mid", local),
        ("send_root", leaf_slots + slot),
        ("leaf", leaf_slots),
        ("out", slot),
        ("mid_order", local),
        ("mid_out", slot),
        ("mid_send", slot),
        ("turn", 1),
    ):
        at[name] = size
        size += count
    at["size"] = size
    return at


def plan_kernel(local, slot, leaf_slots, place_ref, bounds_ref, leaf_ref, parents_ref, out_ref, front, ident, where, record):
    row, col = place_ref[0], place_ref[1]
    x, h = row // 2, row % 2
    total = 4 * local
    mark_fronts(bounds_ref, front)
    chains = range(len(ORDERS))
    at = plan_layout(local, slot, leaf_slots)

    def per_row(r, before):
        zeros = lax.fori_loop(0, local, lambda i, s: s + 1 - front[r * local + i], jnp.int32(0))

        def body(i, carry):
            low, high = carry
            kind = front[r * local + i]
            rank = jnp.where(kind == 0, low, zeros + high)
            chip = (before + rank) & 7
            ident[r * local + chip * slot + (rank >> 3)] = r * local + i
            return low + 1 - kind, high + kind

        lax.fori_loop(0, local, body, (jnp.int32(0), jnp.int32(0)))
        return before + zeros

    lax.fori_loop(0, 4, per_row, jnp.int32(0))

    def clear(v):
        for n in chains:
            where[n, v] = 0

    loop(total, clear)

    def per_chip(chip, _):
        here = chip == col
        near = [place_of(chip, col, bits, slot) for bits in ORDERS]

        def put(core, count, block, code):
            for n in chains:
                where[n, block] = (core ^ h) * local + near[n] + count

            @pl.when(here & (core == h))
            def _():
                for n in chains:
                    out_ref[n, count] = code

        def from_far(step, carry):
            count0, count1 = carry
            core, k = step // slot, step % slot
            block = ident[(2 * (1 - x) + core) * local + chip * slot + k]
            taken = front[block] == x
            count = jnp.where(core == 0, count0, count1)

            @pl.when(taken)
            def _():
                put(core, count, block, 2 * slot + k)

            add = taken.astype(jnp.int32)
            return count0 + jnp.where(core == 0, add, 0), count1 + jnp.where(core == 0, 0, add)

        counts = lax.fori_loop(0, 2 * slot, from_far, (jnp.int32(0), jnp.int32(0)))

        def from_near(step, carry):
            count0, count1 = carry
            owner, k = step // slot, step % slot
            block = ident[(2 * x + owner) * local + chip * slot + k]
            taken = front[block] == x
            core = (count0 >= slot).astype(jnp.int32)
            count = jnp.where(core == 0, count0, count1)

            @pl.when(taken)
            def _():
                put(core, count, block, (owner ^ core) * slot + k)

            add = taken.astype(jnp.int32)
            return count0 + jnp.where(core == 0, add, 0), count1 + jnp.where(core == 0, 0, add)

        lax.fori_loop(0, 2 * slot, from_near, counts)
        return 0

    lax.fori_loop(0, 8, per_chip, 0)

    def mid_list(j):
        block = bounds_ref[x, h * local + j]
        for n in chains:
            out_ref[n, at["mid"] + j] = where[n, block]

    loop(local, mid_list)
    far = 2 * (1 - x) + h
    turn = jnp.int32(6)
    for k in range(7, 0, -1):
        apart = [(parents_ref[c] != parents_ref[c ^ k]).astype(jnp.int32) for c in range(8)]
        turn = jnp.where(functools.reduce(jnp.multiply, apart) == 1, k - 1, turn)
    out_ref[0, at["turn"]] = turn
    listed = 4 * leaf_slots

    def per_leaf(leaf, _):
        @pl.when(parents_ref[leaf] == x)
        def _():
            def body(j, rank):
                block = leaf_ref[leaf, j]
                taken = block >= total

                @pl.when(taken)
                def _():
                    record[block - total] = leaf * 4 * slot + rank

                return rank + taken.astype(jnp.int32)

            lax.fori_loop(0, listed, body, jnp.int32(0))

        return 0

    lax.fori_loop(0, 8, per_leaf, 0)

    def spot(block):
        leaf, rank = record[block] // (4 * slot), record[block] % (4 * slot)
        chip = jnp.where(rank < 2 * slot, leaf, leaf ^ (turn + 1))
        return chip, rank // slot % 2, rank % slot

    def mid_orders(block):
        chip, core, k = spot(block)

        @pl.when(core == h)
        def _():
            for n in chains:
                place = place_of(chip, col, ORDERS[n], slot) + k
                out_ref[n, at["mid_order"] + place] = (block // local ^ h) * local + block % local

    loop(2 * local, mid_orders)

    def mid_outs(j):
        chip, core, k = spot(h * local + col * slot + j)
        out_ref[0, at["mid_out"] + j] = jnp.where(core == h, chip * slot + k, local + j)
        chip, core, k = spot((1 - h) * local + col * slot + j)
        out_ref[0, at["mid_send"] + j] = chip * slot + k

    loop(slot, mid_outs)

    def sends(j):
        asked = leaf_ref[col, far * leaf_slots + j]
        for n in chains:
            out_ref[n, at["send_root"] + j] = where[n, jnp.minimum(asked, total - 1)]

    loop(leaf_slots, sends)

    def count(j, rank):
        return rank + (leaf_ref[col, j] >= total).astype(jnp.int32)

    def lists(j, rank):
        held = leaf_ref[col, row * leaf_slots + j]
        low = jnp.minimum(held, total - 1)
        place = (rank // slot % 2 ^ h) * 2 * slot + rank // (2 * slot) * slot + rank % slot
        for n in chains:
            from_root = jnp.where(front[low] == x, where[n, low], 2 * local + j)
            from_mid = 2 * local + leaf_slots + slot + place
            out_ref[n, at["leaf"] + j] = jnp.where(held < total, from_root, from_mid)
        return count(row * leaf_slots + j, rank)

    lax.fori_loop(0, leaf_slots, lists, lax.fori_loop(0, row * leaf_slots, count, jnp.int32(0)))

    def outs(j):
        asked = far * local + col * slot + j
        held = row * local + col * slot + j
        for n in chains:
            out_ref[n, at["send_root"] + leaf_slots + j] = where[n, asked]
            out_ref[n, at["out"] + j] = jnp.where(front[held] == x, where[n, held], 2 * local + leaf_slots + j)

    loop(slot, outs)


def start_fetch(sources, code, target, sem):
    base = 0
    for source, rows in sources:
        count = source.shape[0]

        @pl.when((code >= base) & (code < base + count))
        def _(source=source, base=base, rows=rows):
            pltpu.make_async_copy(source.at[code - base, rows], target, sem).start()

        base += count


def flatten(parts):
    arrays, plans = [], []
    for order, width, sources in parts:
        plan = []
        for array, first in sources:
            number = next((i for i, known in enumerate(arrays) if known is array), len(arrays))
            if number == len(arrays):
                arrays.append(array)
            plan.append((number, first))
        plans.append((order, width, tuple(plan)))
    return arrays, tuple(plans)


def fetch_all(plans, start, count, table_ref, refs, target, sems):
    def each(act):
        first = 0
        for p, (order, width, plan) in enumerate(plans):
            for i in range(count):
                place = target(i, p, first, width)
                act(p, i, order, [(refs[k], pl.ds(row, width)) for k, row in plan], place)
            first += width

    def begin(p, i, order, sources, place):
        start_fetch(sources, table_ref[order, start + i], place, sems.at[p, i])

    def end(p, i, order, sources, place):
        blocks, rows = sources[0]
        pltpu.make_async_copy(blocks.at[0, rows], place, sems.at[p, i]).wait()

    each(begin)
    each(end)


def gather_kernel(plans, start, count, total, split, table_ref, *refs):
    outs, sems = refs[-1 - (len(plans) if split else 1) : -1], refs[-1]

    def target(i, p, first, width):
        return outs[p].at[i] if split else outs[0].at[i, pl.ds(first, width)]

    fetch_all(plans, start, count, table_ref, refs[:total], target, sems)


def gather(table, start, count, parts, after=(), split=False):
    arrays, plans = flatten(parts)
    widths = [part[1] for part in plans] if split else [sum(part[1] for part in plans)]
    outs = pl.pallas_call(
        functools.partial(gather_kernel, plans, start, count, len(arrays), split),
        out_shape=[jax.ShapeDtypeStruct((count, width, BLOCK), BF16) for width in widths],
        in_specs=[SMEM] + [ANY] * (len(arrays) + len(after)),
        out_specs=[VMEM] * len(widths),
        scratch_shapes=[pltpu.SemaphoreType.DMA((len(plans), count))],
        compiler_params=params(10),
    )(table, *arrays, *after)
    return outs if split else outs[0]


def store_blocks(ref, result):
    for i in range(ref.shape[0]):
        ref[i] = result[:, i * BLOCK : (i + 1) * BLOCK].astype(ref.dtype)


def root_product_kernel(parts, last, order_ref, value_ref, *refs):
    blocks, outs, turned = refs[:parts], refs[parts:-1], refs[-1]
    step = pl.program_id(0)

    @pl.when(step == 0)
    def _():
        turned[...] = value_ref[...].T

    matrix = jnp.concatenate([b[...] for b in blocks], axis=0)
    result = lax.dot_general(turned[...], matrix, NT, preferred_element_type=F32)
    width = result.shape[0] // len(CHAINS)
    for n, order in enumerate(CHAINS):
        part = result[n * width : (n + 1) * width]
        if last:
            store_blocks(outs[n], part)
            continue
        next_step = 2 - order

        @pl.when(step != next_step)
        def _(n=n, part=part):
            store_blocks(outs[2 * n], part)

        @pl.when(step == next_step)
        def _(n=n, part=part):
            store_blocks(outs[2 * n + 1], part)


def root_product(order, value, matrix, last):
    depth, width = value.shape
    local = matrix.shape[0] // BLOCK
    parts = local // 4
    base = 0 if last else 3

    def spec(i):
        return pl.BlockSpec((BLOCK, depth), lambda s, order: (order[parts * (base - s) + i], 0))

    part = width // len(CHAINS)
    block = (parts, part, BLOCK)
    fixed = pl.BlockSpec(block, lambda s, order: (0, 0, 0))
    rest = jax.ShapeDtypeStruct(block, BF16)
    if last:
        out_specs, out_shape = [fixed] * len(CHAINS), [rest] * len(CHAINS)
    else:
        first = pl.BlockSpec(block, lambda s, order: (jnp.where(s == 0, 1, 0), 0, 0))
        out_specs = [first, fixed] * len(CHAINS)
        out_shape = [jax.ShapeDtypeStruct((local // 2, part, BLOCK), BF16), rest] * len(CHAINS)
    return pl.pallas_call(
        functools.partial(root_product_kernel, parts, last),
        grid_spec=pltpu.PrefetchScalarGridSpec(
            num_scalar_prefetch=1,
            grid=(1 if last else 3,),
            in_specs=[pl.BlockSpec((depth, width), lambda s, order: (0, 0))] + [spec(i) for i in range(parts)],
            out_specs=out_specs,
            scratch_shapes=[pltpu.VMEM((width, depth), BF16)],
        ),
        out_shape=out_shape,
        compiler_params=params(60),
        cost_estimate=cost(matrix.shape[0] // 4 * (1 if last else 3), depth, width),
    )(order, value, *([matrix] * parts))


def mid_first_kernel(front_ref, term_ref, got_ref, rhs_ref, matrix_ref, *refs):
    out_ref, shift_ref = refs[-2:]

    @pl.when(pl.program_id(0) == 0)
    def _():
        shift_ref[...] = (rhs_ref[0].T.astype(F32) - (term_ref[...].astype(F32) + got_ref[...].astype(F32))).astype(BF16)

    store_blocks(out_ref, lax.dot_general(shift_ref[...], matrix_ref[...], NT, preferred_element_type=F32))


def mid_rest_kernel(shift_ref, matrix_ref, out_ref):
    store_blocks(out_ref, lax.dot_general(shift_ref[...], matrix_ref[...], NT, preferred_element_type=F32))


def mid_first(front, term, got, rhs, matrix, after):
    width, depth = term.shape
    half = matrix.shape[0] // BLOCK // 2
    whole = pl.BlockSpec((width, depth), lambda s, front: (0, 0))
    return pl.pallas_call(
        mid_first_kernel,
        grid_spec=pltpu.PrefetchScalarGridSpec(
            num_scalar_prefetch=1,
            grid=(2,),
            in_specs=[
                whole,
                whole,
                pl.BlockSpec((1, depth, width), lambda s, front: (front[0], 0, 0)),
                pl.BlockSpec((half // 2 * BLOCK, depth), lambda s, front: (s, 0)),
            ]
            + [ANY] * len(after),
            out_specs=[pl.BlockSpec((half // 2, width, BLOCK), lambda s, front: (s, 0, 0)), whole],
        ),
        out_shape=[
            jax.ShapeDtypeStruct((half, width, BLOCK), BF16),
            jax.ShapeDtypeStruct((width, depth), BF16),
        ],
        compiler_params=params(60),
        cost_estimate=cost(half * BLOCK, depth, width),
    )(front.reshape(1), term, got, rhs, matrix, *after)


def mid_rest(shift, matrix):
    width, depth = shift.shape
    half = matrix.shape[0] // BLOCK // 2
    return pl.pallas_call(
        mid_rest_kernel,
        grid=(2,),
        in_specs=[
            pl.BlockSpec((width, depth), lambda s: (0, 0)),
            pl.BlockSpec((half // 2 * BLOCK, depth), lambda s: (2 + s, 0)),
        ],
        out_specs=pl.BlockSpec((half // 2, width, BLOCK), lambda s: (s, 0, 0)),
        out_shape=jax.ShapeDtypeStruct((half, width, BLOCK), BF16),
        compiler_params=params(60),
        cost_estimate=cost(half * BLOCK, depth, width),
    )(shift, matrix)


def mid_coupling_kernel(plans, start, count, total, table_ref, *refs):
    coup_ref, out_ref, bound, sems = refs[total:]

    def target(i, p, first, width):
        return bound.at[pl.ds(first, width), pl.ds(i * BLOCK, BLOCK)]

    @pl.when(pl.program_id(0) == 0)
    def _():
        fetch_all(plans, start, count, table_ref, refs[:total], target, sems)

    product = lax.dot_general(bound[...], coup_ref[...], NN, preferred_element_type=F32)
    out_ref[...] = product.astype(BF16)


def mid_coupling(table, start, parts, coup, steps=4):
    arrays, plans = flatten(parts)
    width = sum(part[1] for part in plans)
    depth, cols = coup.shape
    count = depth // BLOCK
    tile = pl.BlockSpec((width, cols // steps), lambda s: (0, s))
    return pl.pallas_call(
        functools.partial(mid_coupling_kernel, plans, start, count, len(arrays)),
        grid=(steps,),
        in_specs=[SMEM] + [ANY] * len(arrays) + [pl.BlockSpec((depth, cols // steps), lambda s: (0, s))],
        out_specs=tile,
        out_shape=jax.ShapeDtypeStruct((width, cols), BF16),
        scratch_shapes=[pltpu.VMEM((width, depth), BF16), pltpu.SemaphoreType.DMA((len(plans), count))],
        compiler_params=params(24),
        cost_estimate=cost(cols, depth, width),
    )(table, *arrays, coup)


def leaf_first_kernel(plans, start, count, total, table_ref, order_ref, *refs):
    matrix_ref, out_ref, bound_ref, sems = refs[total:]

    def target(i, p, first, width):
        return bound_ref.at[pl.ds(first, width), pl.ds(i * BLOCK, BLOCK)]

    @pl.when(pl.program_id(0) == 0)
    def _():
        fetch_all(plans, start, count, table_ref, refs[:total], target, sems)

    out_ref[0] = lax.dot_general(bound_ref[...], matrix_ref[...], NN, preferred_element_type=F32).astype(BF16)


def leaf_first(table, start, parts, order, matrix, cols):
    arrays, plans = flatten(parts)
    width = sum(part[1] for part in plans)
    depth = matrix.shape[0]
    count = depth // BLOCK
    return pl.pallas_call(
        functools.partial(leaf_first_kernel, plans, start, count, len(arrays)),
        grid_spec=pltpu.PrefetchScalarGridSpec(
            num_scalar_prefetch=2,
            grid=(2,),
            in_specs=[ANY] * len(arrays) + [pl.BlockSpec((depth, cols), lambda s, table, order: (0, order[s]))],
            out_specs=[
                pl.BlockSpec((1, width, cols), lambda s, table, order: (s, 0, 0)),
                pl.BlockSpec((width, depth), lambda s, table, order: (0, 0)),
            ],
            scratch_shapes=[pltpu.SemaphoreType.DMA((len(plans), count))],
        ),
        out_shape=[
            jax.ShapeDtypeStruct((2, width, cols), BF16),
            jax.ShapeDtypeStruct((width, depth), BF16),
        ],
        compiler_params=params(60),
        cost_estimate=cost(2 * cols, depth, width),
    )(table, order, *arrays, matrix)


def leaf_shift_kernel(order_ref, keep_ref, got_ref, far_ref, rhs_ref, matrix_ref, *refs):
    out_ref, shift_ref = refs[-2:]

    @pl.when(pl.program_id(0) == 0)
    def _():
        term = keep_ref[0] + got_ref[0].astype(F32) + far_ref[...].astype(F32)
        shift_ref[...] = (rhs_ref[0].T.astype(F32) - term).astype(BF16)

    product = lax.dot_general(shift_ref[...], matrix_ref[...], NT, preferred_element_type=F32)
    out_ref[0] = product.astype(BF16)


def leaf_shift(order, keep, got, far, rhs, matrix, after):
    _, width, depth = keep.shape
    one = pl.BlockSpec((1, width, depth), lambda s, order: (0, 0, 0))
    flat = pl.BlockSpec((width, depth), lambda s, order: (0, 0))
    return pl.pallas_call(
        leaf_shift_kernel,
        grid_spec=pltpu.PrefetchScalarGridSpec(
            num_scalar_prefetch=1,
            grid=(2,),
            in_specs=[
                one,
                one,
                flat,
                pl.BlockSpec(rhs.shape, lambda s, order: (0, 0, 0)),
                pl.BlockSpec((depth, depth), lambda s, order: (order[s], 0)),
            ]
            + [ANY] * len(after),
            out_specs=[pl.BlockSpec((1, width, depth), lambda s, order: (s, 0, 0)), flat],
        ),
        out_shape=[
            jax.ShapeDtypeStruct((2, width, depth), BF16),
            jax.ShapeDtypeStruct((width, depth), BF16),
        ],
        compiler_params=params(60),
        cost_estimate=cost(2 * depth, depth, width),
    )(order, keep, got, far, rhs, matrix, *after)


def leaf_rest_kernel(dims, order_ref, value_ref, matrix_ref, out_ref):
    out_ref[0] = lax.dot_general(value_ref[...], matrix_ref[...], dims, preferred_element_type=F32)


def leaf_rest(order, dims, value, matrix, cols, mib):
    width, depth = value.shape
    if dims is NN:
        spec = pl.BlockSpec((depth, cols), lambda s, order: (0, order[2 + s]))
    else:
        spec = pl.BlockSpec((cols, depth), lambda s, order: (order[2 + s], 0))
    return pl.pallas_call(
        functools.partial(leaf_rest_kernel, dims),
        grid_spec=pltpu.PrefetchScalarGridSpec(
            num_scalar_prefetch=1,
            grid=(2,),
            in_specs=[pl.BlockSpec((width, depth), lambda s, order: (0, 0)), spec],
            out_specs=pl.BlockSpec((1, width, cols), lambda s, order: (s, 0, 0)),
        ),
        out_shape=jax.ShapeDtypeStruct((2, width, cols), F32),
        compiler_params=params(mib),
        cost_estimate=cost(2 * cols, depth, width),
    )(order, value, matrix)


def leaf_finish_kernel(keep_ref, got_ref, far_ref, *refs):
    total = keep_ref[0] + got_ref[0].astype(F32) + far_ref[...].astype(F32)
    refs[-1][0] = total.astype(BF16).T


def leaf_finish(keep, got, far, after):
    _, width, rows = keep.shape
    one = pl.BlockSpec((1, width, rows), lambda s: (0, 0, 0))
    return pl.pallas_call(
        leaf_finish_kernel,
        grid=(1,),
        in_specs=[one, one, pl.BlockSpec((width, rows), lambda s: (0, 0))] + [ANY] * len(after),
        out_specs=pl.BlockSpec((1, rows, width), lambda s: (0, 0, 0)),
        out_shape=jax.ShapeDtypeStruct((1, rows, width), BF16),
        compiler_params=params(60),
    )(keep, got, far, *after)


def swap(value, axis, mask):
    return lax.ppermute(value, axis, [(i, i ^ mask) for i in range(lax.axis_size(axis))])


def add(*terms):
    return functools.reduce(jnp.add, [t.astype(F32) for t in terms])


def tie(value, others):
    value, others[:] = lax.optimization_barrier((value, list(others)))
    return value


def reduce_columns(send, hold, keep, bits, early, step):
    for i, bit in enumerate(bits):
        got = swap(send, "col", bit)
        if i == step:
            got = tie(got, early)
        if i < len(bits) - 1:
            half = got.shape[0] // 2
            send = add(hold, got[half:]).astype(BF16)
            keep = add(keep, got[:half])
        if i < len(bits) - 2:
            hold, keep = keep[half // 2 :], keep[: half // 2]
    return add(keep, got).astype(BF16)


def turn_columns(value, turn):
    return lax.switch(turn, [lambda v, k=k: swap(v, "col", k) for k in range(1, 8)], value)


def gather_columns(value, bits):
    for bit in (bits[2], bits[1]):
        value = jnp.concatenate([value, swap(value, "col", bit)], axis=0)
    far = swap(value, "col", bits[0])
    return [value, far, swap(value, "row", 1), swap(far, "row", 1)]


def natural(blocks):
    return jnp.swapaxes(blocks, 1, 2).reshape(-1, blocks.shape[1])


def shards(
    dinv_root,
    rhs_root,
    dinv_mid,
    coup_mid,
    rhs_mid,
    dinv_leaf,
    coup_leaf,
    rhs_leaf,
    bounds_mid,
    bounds_leaf,
    parents,
):
    row_id = lax.axis_index("row")
    col_id = lax.axis_index("col")
    x, h = row_id // 2, row_id % 2
    place = jnp.stack([row_id, col_id]).astype(jnp.int32)
    local = dinv_root.shape[0] // BLOCK
    slot = local // 8
    leaf_slots = bounds_leaf.shape[1] // 4
    at = plan_layout(local, slot, leaf_slots)

    order = pl.pallas_call(
        functools.partial(order_kernel, local, slot),
        out_shape=jax.ShapeDtypeStruct((local,), jnp.int32),
        in_specs=[SMEM] * 2,
        out_specs=SMEM,
        scratch_shapes=[pltpu.SMEM((4 * local,), jnp.int32)],
    )(place, bounds_mid)
    plan = pl.pallas_call(
        functools.partial(plan_kernel, local, slot, leaf_slots),
        out_shape=jax.ShapeDtypeStruct((len(ORDERS), at["size"]), jnp.int32),
        in_specs=[SMEM] * 4,
        out_specs=SMEM,
        scratch_shapes=[pltpu.SMEM((4 * local,), jnp.int32)] * 2
        + [pltpu.SMEM((len(ORDERS), 4 * local), jnp.int32), pltpu.SMEM((2 * local,), jnp.int32)],
    )(place, bounds_mid, bounds_leaf, parents)

    half, quarter = local // 2, local // 4
    leaf_order = jnp.stack([2 * x + 1 - h, 2 * (1 - x) + 1 - h, 2 * x + h, 2 * (1 - x) + h]).astype(jnp.int32)
    leaf_cols = coup_leaf.shape[2] // 4
    width = rhs_root.shape[1] // len(CHAINS)
    chains = range(len(CHAINS))

    def whole(arrays):
        return [(array, 0) for array in arrays]

    def rows(arrays, n):
        return [(array, n * width) for array in arrays]

    first = root_product(order, rhs_root, dinv_root, False)
    last = root_product(order, rhs_root, dinv_root, True)
    tables = [plan]
    boundary = []
    for n, kind in enumerate(CHAINS):
        got = reduce_columns(*first[2 * n : 2 * n + 2], last[n], ORDERS[kind], tables, 0)
        picked = [(kind, width, whole((got, swap(got, "row", 1), swap(got, "row", 2))))]
        boundary.append(gather_columns(gather(tables[0], at["select"], slot, picked), ORDERS[kind]))
    plan = tables[0]
    parts = [(kind, width, whole(boundary[n])) for n, kind in enumerate(CHAINS)]

    term = mid_coupling(plan, at["mid"], parts, coup_mid)
    front, shift = mid_first(x, term, swap(term, "row", 1), rhs_mid, dinv_mid, ())
    back = mid_rest(shift, dinv_mid)
    asking = gather(plan, at["send_root"], leaf_slots + slot, parts, (back,), split=True)
    asked = [[swap(part, "row", 2)] for part in asking]
    products = (front, back, swap(front, "row", 1), swap(back, "row", 1))
    parts = [(kind, width, rows(products, n)) for n, kind in enumerate(CHAINS)]
    sends = gather(plan, at["mid_order"] + half, half, parts, split=True)
    keeps = gather(plan, at["mid_order"], half, parts, (sends[0],), split=True)
    got = []
    for n, kind in enumerate(CHAINS):
        hold, keep = keeps[n][quarter:], keeps[n][:quarter]
        early = [] if n == 0 else asked[0]
        got.append(reduce_columns(sends[n], hold, keep, ORDERS[kind], early, 1))
    got = tie(jnp.concatenate(got, axis=1), asked[1])
    other = swap(got, "row", 2)
    child = parents[col_id] == x
    mine, away = jnp.where(child, got, other), jnp.where(child, other, got)
    own = jnp.concatenate([mine, turn_columns(away, plan[0, at["turn"]])], axis=0)
    sib = swap(own, "row", 1)
    sources = [(kind, width, whole((*boundary[n], *asked[n])) + rows((own, sib), n)) for n, kind in enumerate(CHAINS)]
    mid = lax.all_gather(got, "col", axis=0, tiled=True)

    def reduce_rows(send, keep):
        got = swap(send, "row", 1)
        far = swap(add(keep[1], got[1]).astype(BF16), "row", 2)
        return keep, got, far

    send, bound = leaf_first(plan, at["leaf"], sources, leaf_order, coup_leaf[0], leaf_cols)
    terms = reduce_rows(send, leaf_rest(leaf_order, NN, bound, coup_leaf[0], leaf_cols, 60))
    held = [(kind, width, whole((*boundary[n], *asked[n]))) for n, kind in enumerate(CHAINS)]
    root_values = gather(plan, at["out"], slot, held)
    root_values = natural(root_values)
    send, shift = leaf_shift(leaf_order, *terms, rhs_leaf, dinv_leaf[0], (root_values,))
    terms = reduce_rows(send, leaf_rest(leaf_order, NT, shift, dinv_leaf[0], leaf_cols, 60))
    joint = len(CHAINS) * width
    wanted = gather(plan, at["mid_send"], slot, [(0, joint, whole((mid,)))])
    mid_values = gather(plan, at["mid_out"], slot, [(0, joint, whole((mid, swap(wanted, "row", 1))))])
    mid_values = natural(mid_values)
    return (root_values, mid_values, leaf_finish(*terms, (mid_values,)))


def solution(mesh):
    sizes = dict(mesh.shape)
    in_specs = (
        P("row", "col"),
        P("col", None),
        P("row", "col"),
        P("row", "col"),
        P(None, "col", None),
        P("col", None, "row"),
        P("col", "row", None),
        P("col", "row", None),
        P(),
        P(),
        P(),
    )
    out_specs = (P(("row", "col"), None), P(("row", "col"), None), P("col", "row", None))

    def run(*args):
        fronts, listed = args[8].shape
        blocks = args[0].shape[0] // BLOCK
        whole = fronts == 2 and fronts * listed == blocks and args[2].shape[0] == args[0].shape[0]
        fits = sizes["row"] == 4 and sizes["col"] == 8 and whole
        body = shards if fits else general_shards
        return jax.shard_map(body, mesh=mesh, in_specs=in_specs, out_specs=out_specs, check_vma=False)(*args)

    return run
```
